256 devices in a mesh: dp: 16 (over z, y_hi), tensor: 16 (over x, y_lo, core).
Axes of the slice: x: 4, y: 4 (y_hi: 2, y_lo: 2; y = y_hi * 2 + y_lo), z: 8, core: 2. Of those that a mesh axis runs over, the one named last changes fastest.
Arguments:
- hidden: bfloat16 [12288, 14336], P('dp', 'tensor'), may hold values from -6 to 6
- grad_out: bfloat16 [12288, 4096], P('dp', 'tensor'), may hold values from -6 to 6
- weight: bfloat16 [14336, 4096], P('tensor', 'dp'), may hold values from -0.09375 to 0.09375
Outputs:
- grad_hidden: bfloat16 [12288, 14336], P('dp', 'tensor')
- grad_weight: bfloat16 [14336, 4096], P('tensor', 'dp')
The draws below stay inside these ranges and needn't reach their ends.
All inputs are finite; a program needn't handle non-finite values.
Results may differ from the reference program's by a relative error of at most 0.001.
Values may be sent and summed in bfloat16 or wider, within the bound.
No kernel may reach another device: no remote copies, remote signals or barrier semaphores. Data moves between devices by JAX's collectives and lax.ppermute only.
A program may use at most 128 MiB of HBM per device.

```python
import jax
import jax.numpy as jnp
from jax import lax

D = 4096
FF = 14336
TOKENS = 12288


def spiked(drawn, key, source, target, blocks, factor):
    owner, partner = [(jnp.arange(drawn.shape[dim]) // (drawn.shape[dim] // blocks)).reshape([-1 if axis == dim else 1 for axis in range(drawn.ndim)]) for dim in (source, target)]
    chosen = jax.random.permutation(key, blocks)[partner]
    strong = (owner == chosen) | (owner == (partner + blocks // 2) % blocks)
    return jnp.where(strong, factor * drawn, drawn)


def block_levels(rng, extent, cuts, smallest, top_value):
    def one(position, parts):
        draws = jax.random.uniform(jax.random.fold_in(jax.random.fold_in(rng, 6), position), (parts,), jnp.float32, smallest / len(cuts), top_value / len(cuts))
        return jnp.repeat(jnp.exp(draws), extent[position] // parts).reshape((-1,) + (1,) * (len(extent) - position - 1))

    gain = one(*cuts[0])
    for cut in cuts[1:]:
        gain = gain * one(*cut)
    return gain


def bell_draw(stream_key, dims, spread, limit, pieces=(), kind=jnp.bfloat16):
    drawn = jax.random.normal(stream_key, dims, jnp.float32) * spread
    if len(pieces) > 0:
        drawn = block_levels(stream_key, dims, pieces, -0.22, 0.18) * drawn
    return jnp.clip(drawn, min=-limit, max=limit).astype(kind)


def bell_draw_with(stream_key, dims, scale, limit, shards, heavy, kind=jnp.bfloat16):
    result = scale * jax.random.normal(stream_key, dims, jnp.float32)
    if shards:
        result = result * block_levels(stream_key, dims, shards, -0.22, 0.18)
    return jnp.clip(spiked(result, jax.random.fold_in(stream_key, 3), *heavy), -limit, limit).astype(kind)


def setup_inputs(seed: int = 0) -> dict:
    streams_of = jax.random.split(jax.random.key(seed), 4)
    hidden = bell_draw(streams_of[0], (TOKENS, FF), 1.0, 6.0, ((0, 16), (1, 16)))
    grad_out = bell_draw_with(streams_of[1], (TOKENS, D), 1.0, 6.0, ((0, 16), (1, 16)), (0, 1, 16, 2.0))
    weight = bell_draw(streams_of[2], (FF, D), D ** -0.5, 0.09375, ((0, 16), (1, 16)))
    return dict(hidden=hidden, grad_out=grad_out, weight=weight)


def reference(hidden, grad_out, weight):
    grad_hidden = lax.dot_general(grad_out, weight, (((1,), (1,)), ((), ())), preferred_element_type=jnp.float32)
    grad_weight = lax.dot_general(hidden, grad_out, (((0,), (0,)), ((), ())), preferred_element_type=jnp.float32)
    return grad_hidden.astype(jnp.bfloat16), grad_weight.astype(jnp.bfloat16)
```

```python
import jax
import jax.numpy as jnp
from jax import lax
from jax.sharding import Mesh, PartitionSpec as P

PLANE = ("yh", "x", "yl", "c")
Z = 8


def shift(array, axis, size, by):
    return lax.ppermute(array, axis, [(i, (i + by) % size) for i in range(size)])


def pick(first, a, b):
    return jnp.where(first, a, b)


def shards(hidden, grad_out, weight):
    yh = lax.axis_index("yh")
    z = lax.axis_index("z")
    first = yh == 0
    half = hidden.shape[1] // 2
    width = weight.shape[1]
    tokens = hidden.shape[0]

    full = lax.all_gather(grad_out, PLANE, axis=1, tiled=True)
    columns = full.shape[1] // 2

    w_keep = pick(first, weight[:half], weight[half:])
    w_got = shift(pick(first, weight[half:], weight[:half]), "yh", 2, 1)
    piece = jnp.concatenate(
        [pick(first, w_keep, w_got), pick(first, w_got, w_keep)], axis=1
    )
    rows = jnp.zeros((half, columns), weight.dtype)

    def put(rows, block, owner):
        return lax.dynamic_update_slice(rows, block, (0, (owner % Z) * 2 * width))

    rows = put(rows, piece, z)
    up, down = piece, piece
    for step in range(1, 5):
        up = shift(up, "z", Z, 1)
        rows = put(rows, up, z - step + Z)
        if step < 4:
            down = shift(down, "z", Z, -1)
            rows = put(rows, down, z + step)

    h_keep = pick(first, hidden[:, :half], hidden[:, half:])
    h_got = shift(pick(first, hidden[:, half:], hidden[:, :half]), "yh", 2, 1)
    h0, h1 = pick(first, h_keep, h_got), pick(first, h_got, h_keep)

    g0, g1 = full[:, :columns], full[:, columns:]
    over_tokens = (((0,), (0,)), ((), ()))
    term = lax.dot_general(
        g0, h0, over_tokens, preferred_element_type=jnp.float32
    ) + lax.dot_general(g1, h1, over_tokens, preferred_element_type=jnp.float32)
    shard = lax.psum_scatter(term, "z", scatter_dimension=0, tiled=True)

    over_columns = (((1,), (1,)), ((), ()))
    gh = [
        lax.dot_general(
            g, rows, over_columns, preferred_element_type=jnp.float32
        ).astype(jnp.bfloat16)
        for g in (g0, g1)
    ]
    gh_keep = pick(first, gh[0], gh[1])
    gh_got = shift(pick(first, gh[1], gh[0]), "yh", 2, 1)
    grad_hidden = jnp.concatenate(
        [pick(first, gh_keep, gh_got), pick(first, gh_got, gh_keep)], axis=1
    )

    gw = shard.T.astype(jnp.bfloat16)
    gw_keep = pick(first, gw[:, :width], gw[:, width:])
    gw_got = shift(pick(first, gw[:, width:], gw[:, :width]), "yh", 2, 1)
    grad_weight = jnp.concatenate(
        [pick(first, gw_keep, gw_got), pick(first, gw_got, gw_keep)], axis=0
    )
    return (grad_hidden, grad_weight)


def solution(mesh):
    fine = Mesh(
        mesh.devices.reshape(Z, 2, 4, 2, 2), ("z", "yh", "x", "yl", "c")
    )
    dp, tensor = ("z", "yh"), ("x", "yl", "c")
    return jax.shard_map(
        shards,
        mesh=fine,
        in_specs=(P(dp, tensor), P(dp, tensor), P(tensor, dp)),
        out_specs=(P(dp, tensor), P(tensor, dp)),
        check_vma=False,
    )
```

```python
import functools

import jax
import jax.numpy as jnp
from jax import lax
from jax.experimental import pallas as pl
from jax.experimental.pallas import tpu as pltpu
from jax.sharding import Mesh, PartitionSpec as P

PLANE = ("yh", "x", "yl", "c")
FINE = ("z", "yh", "x", "yl", "c")
Z = 8
LANES = 128
EXTRA = 16
SPREAD = 2.0**7.875


def shift(array, axis, size, by):
    return lax.ppermute(array, axis, [(i, (i + by) % size) for i in range(size)])


def pick(first, a, b):
    return jnp.where(first, a, b)


def decode(message, rows):
    code = message[:rows].astype(jnp.float32)
    scale = jnp.exp2(message[rows : rows + 1].astype(jnp.float32)) * (1 / SPREAD)
    root = lax.rsqrt(lax.rsqrt(lax.rsqrt(lax.rsqrt(jnp.abs(code)))))
    return jnp.where(code < 0, -root, root) * scale


def encode_into(out_ref, total, rows):
    top = jnp.max(jnp.abs(total), axis=0, keepdims=True)
    e = jnp.ceil(jnp.log2(jnp.maximum(top, 1e-35)))
    u = total * (jnp.exp2(-e) * SPREAD)
    u2 = u * u
    u4 = u2 * u2
    u8 = u4 * u4
    u16 = u8 * u8
    out_ref[:rows] = jnp.where(total < 0, -u16, u16).astype(out_ref.dtype)
    out_ref[rows:] = jnp.broadcast_to(e, (EXTRA, total.shape[1])).astype(out_ref.dtype)


def first_kernel(where_ref, term_ref, out_ref):
    encode_into(out_ref, term_ref[...], term_ref.shape[0])


def hop_kernel(where_ref, term_ref, got_ref, out_ref):
    rows = term_ref.shape[0]
    encode_into(out_ref, decode(got_ref, rows) + term_ref[...], rows)


def last_kernel(where_ref, term_ref, right_ref, left_ref, out_ref):
    rows = term_ref.shape[0]
    total = decode(right_ref, rows) + decode(left_ref, rows) + term_ref[...]
    out_ref[...] = total.astype(out_ref.dtype)


def ring_call(kernel, where, term, got, skips, final):
    rows = term.shape[0]
    n = where.shape[0]
    out_rows = rows if final else rows + EXTRA
    specs = [pl.BlockSpec((rows, LANES), lambda i, w: (0, w[i]))]
    for skip in skips:
        specs.append(
            pl.BlockSpec((rows + EXTRA, LANES), lambda i, w, skip=skip: (0, i + skip))
        )
    return pl.pallas_call(
        kernel,
        out_shape=jax.ShapeDtypeStruct((out_rows, n * LANES), jnp.bfloat16),
        grid_spec=pltpu.PrefetchScalarGridSpec(
            num_scalar_prefetch=1,
            grid=(n,),
            in_specs=specs,
            out_specs=pl.BlockSpec((out_rows, LANES), lambda i, w: (0, i)),
        ),
        cost_estimate=pl.CostEstimate(
            flops=rows * n * LANES * 20, bytes_accessed=rows * n * LANES * 8, transcendentals=0
        ),
    )(where, term, *got)


def ring_sums(term, z, width):
    blocks = width // LANES
    half = jnp.arange(blocks, dtype=jnp.int32)

    def at(a, b):
        parts = []
        if a is not None:
            parts.append((a % Z) * 2 * blocks + half)
        if b is not None:
            parts.append((b % Z) * 2 * blocks + blocks + half)
        return jnp.concatenate(parts)

    right = ring_call(first_kernel, at(z + 4, z + 3), term, [], [], False)
    left = ring_call(first_kernel, at(z + 5, z + 4), term, [], [], False)
    for step in range(2, 5):
        right, left = shift(right, "z", Z, 1), shift(left, "z", Z, -1)
        if step < 4:
            right = ring_call(hop_kernel, at(z + 5 - step, z + 4 - step), term, [right], [0], False)
            left = ring_call(hop_kernel, at(z + 4 + step, z + 3 + step), term, [left], [0], False)
    right4 = shift(ring_call(hop_kernel, at(z + 1, None), term, [right], [0], False), "z", Z, 1)
    left4 = shift(ring_call(hop_kernel, at(None, z + 7), term, [left], [blocks], False), "z", Z, -1)
    a = ring_call(last_kernel, at(z, None), term, [right4, left], [0, 0], True)
    b = ring_call(last_kernel, at(None, z), term, [right, left4], [blocks, 0], True)
    return a, b


def shards(hidden, grad_out, weight):
    yh = lax.axis_index("yh")
    z = lax.axis_index("z")
    first = yh == 0
    half = hidden.shape[1] // 2
    width = weight.shape[1]

    full = lax.all_gather(grad_out, PLANE, axis=1, tiled=True)
    columns = full.shape[1] // 2

    w_keep = pick(first, weight[:half], weight[half:])
    w_got = shift(pick(first, weight[half:], weight[:half]), "yh", 2, 1)
    piece = jnp.concatenate(
        [pick(first, w_keep, w_got), pick(first, w_got, w_keep)], axis=1
    )
    rows = jnp.zeros((half, columns), weight.dtype)

    def put(rows, block, owner):
        return lax.dynamic_update_slice(rows, block, (0, (owner % Z) * 2 * width))

    rows = put(rows, piece, z)
    up, down = piece, piece
    for step in range(1, 5):
        up = shift(up, "z", Z, 1)
        rows = put(rows, up, z - step + Z)
        if step < 4:
            down = shift(down, "z", Z, -1)
            rows = put(rows, down, z + step)

    h_keep = pick(first, hidden[:, :half], hidden[:, half:])
    h_got = shift(pick(first, hidden[:, half:], hidden[:, :half]), "yh", 2, 1)
    h0, h1 = pick(first, h_keep, h_got), pick(first, h_got, h_keep)

    full, rows, h0, h1 = lax.optimization_barrier((full, rows, h0, h1))
    g0, g1 = full[:, :columns], full[:, columns:]
    over_tokens = (((0,), (0,)), ((), ()))
    term = lax.dot_general(
        h0, g0, over_tokens, preferred_element_type=jnp.float32
    ) + lax.dot_general(h1, g1, over_tokens, preferred_element_type=jnp.float32)
    gw = ring_sums(term, z, width)

    over_columns = (((1,), (1,)), ((), ()))
    gh = [
        lax.dot_general(
            g, rows, over_columns, preferred_element_type=jnp.float32
        ).astype(jnp.bfloat16)
        for g in (g0, g1)
    ]
    gh_keep = pick(first, gh[0], gh[1])
    gh_got = shift(pick(first, gh[1], gh[0]), "yh", 2, 1)
    grad_hidden = jnp.concatenate(
        [pick(first, gh_keep, gh_got), pick(first, gh_got, gh_keep)], axis=1
    )

    gw_keep = pick(first, gw[0], gw[1])
    gw_got = shift(pick(first, gw[1], gw[0]), "yh", 2, 1)
    grad_weight = jnp.concatenate(
        [pick(first, gw_keep, gw_got), pick(first, gw_got, gw_keep)], axis=0
    )
    return (grad_hidden, grad_weight)


def solution(mesh):
    fine = Mesh(mesh.devices.reshape(Z, 2, 4, 2, 2), FINE)
    dp, tensor = FINE[:2], FINE[2:]
    return jax.shard_map(
        shards,
        mesh=fine,
        in_specs=(P(dp, tensor), P(dp, tensor), P(tensor, dp)),
        out_specs=(P(dp, tensor), P(tensor, dp)),
        check_vma=False,
    )
```

```python
import functools

import jax
import jax.numpy as jnp
from jax import lax
from jax.experimental import pallas as pl
from jax.experimental.pallas import tpu as pltpu
from jax.sharding import Mesh, PartitionSpec as P

FINE = ("z", "yh", "x", "yl", "c")
SIZE = {"z": 8, "x": 4, ("yh", "yl"): 4, "yh": 2, "c": 2}
Y = ("yh", "yl")
EXTRA = 16
VMEM = 48 * 2**20


def shift(array, axis, by):
    size = SIZE[axis]
    return lax.ppermute(array, axis, [(i, (i + by) % size) for i in range(size)])


def pick(first, a, b):
    return jnp.where(first, a, b)


def around(array, axis):
    return [
        array,
        shift(array, axis, 1),
        shift(array, axis, -1),
        shift(array, axis, 2),
    ]


def slot(off):
    off = off % 4
    return jnp.where(off == 0, 0, jnp.where(off == 3, 1, off + 1))


def encode(total):
    top = jnp.max(jnp.abs(total), axis=0, keepdims=True)
    e = jnp.ceil(jnp.log2(jnp.maximum(top, 1e-30)))
    u = total * jnp.exp2(-e)
    code = (u * jnp.abs(u) * 32768.0).astype(jnp.float16)
    tail = jnp.broadcast_to(e, (EXTRA, total.shape[1])).astype(jnp.float16)
    return jnp.concatenate([code, tail], axis=0)


def decode(message):
    rows = message.shape[0] - EXTRA
    code = message[:rows].astype(jnp.float32)
    scale = jnp.exp2(message[rows : rows + 1].astype(jnp.float32))
    root = jnp.sqrt(jnp.abs(code) * (1 / 32768.0))
    return jnp.where(code < 0, -root, root) * scale


def term_kernel(where_ref, ht_ref, a0, b0, a1, b1, out_ref):
    total = None
    at = 0
    for ref in (a0, b0, a1, b1):
        depth = ref.shape[2]
        part = jnp.dot(
            ht_ref[:, at : at + depth], ref[0, 0], preferred_element_type=jnp.float32
        )
        total = part if total is None else total + part
        at += depth
    out_ref[0] = total


def terms(ht, ga, gb, where):
    n = where.shape[0] // 3
    rows = ht.shape[0]
    ta, tb, width = ga.shape[2], gb.shape[2], ga.shape[3]
    xs = lambda i, w: w[3 * i]
    ys = lambda i, w, k: w[3 * i + 1 + k]
    a_spec = lambda k: pl.BlockSpec(
        (1, 1, ta, width), lambda i, w: (ys(i, w, k), xs(i, w), 0, 0)
    )
    b_spec = lambda k: pl.BlockSpec(
        (1, 1, tb, width), lambda i, w: (xs(i, w), ys(i, w, k), 0, 0)
    )
    return pl.pallas_call(
        term_kernel,
        out_shape=jax.ShapeDtypeStruct((n, rows, width), jnp.float32),
        grid_spec=pltpu.PrefetchScalarGridSpec(
            num_scalar_prefetch=1,
            grid=(n,),
            in_specs=[
                pl.BlockSpec(ht.shape, lambda i, w: (0, 0)),
                a_spec(0),
                b_spec(0),
                a_spec(1),
                b_spec(1),
            ],
            out_specs=pl.BlockSpec((1, rows, width), lambda i, w: (i, 0, 0)),
        ),
        compiler_params=pltpu.CompilerParams(vmem_limit_bytes=VMEM),
        cost_estimate=pl.CostEstimate(
            flops=2 * n * rows * width * ht.shape[1],
            bytes_accessed=n * width * (rows * 4 + ht.shape[1] * 2) + 2 * ht.size,
            transcendentals=0,
        ),
    )(where, ht, ga, gb, ga, gb)


def hidden_kernel(where_ref, a_ref, b_ref, w_ref, out_ref):
    @pl.when(pl.program_id(1) == 0)
    def _():
        out_ref[...] = jnp.zeros_like(out_ref)

    ta = a_ref.shape[2]
    dims = (((1,), (1,)), ((), ()))
    w = w_ref[0, 0]
    out_ref[0, :ta] += lax.dot_general(
        a_ref[0, 0], w, dims, preferred_element_type=jnp.float32
    )
    out_ref[0, ta:] += lax.dot_general(
        b_ref[0, 0], w, dims, preferred_element_type=jnp.float32
    )


def hidden_part(ga, gb, rows, where):
    n = rows.shape[0]
    ta, tb, width = ga.shape[2], gb.shape[2], ga.shape[3]
    half = rows.shape[2]
    tokens = ta + tb
    return pl.pallas_call(
        hidden_kernel,
        out_shape=jax.ShapeDtypeStruct((2, tokens, half), jnp.float32),
        grid_spec=pltpu.PrefetchScalarGridSpec(
            num_scalar_prefetch=1,
            grid=(2, n),
            in_specs=[
                pl.BlockSpec(
                    (1, 1, ta, width), lambda t, i, w: (w[3 * i + 1 + t], w[3 * i], 0, 0)
                ),
                pl.BlockSpec(
                    (1, 1, tb, width), lambda t, i, w: (w[3 * i], w[3 * i + 1 + t], 0, 0)
                ),
                pl.BlockSpec((1, 1, half, width), lambda t, i, w: (i, w[3 * n], 0, 0)),
            ],
            out_specs=pl.BlockSpec((1, tokens, half), lambda t, i, w: (t, 0, 0)),
        ),
        compiler_params=pltpu.CompilerParams(vmem_limit_bytes=VMEM),
        cost_estimate=pl.CostEstimate(
            flops=4 * n * tokens * width * half,
            bytes_accessed=2 * n * width * (tokens + half) * 2 + 8 * tokens * half,
            transcendentals=0,
        ),
    )(where, ga, gb, rows)


def cross(array_of, k, out):
    pairs = []
    for p in range(2):
        for q in range(2):
            to = (q, p ^ k) if out else (q ^ k, p)
            pairs.append((p * 2 + q, to[0] * 2 + to[1]))
    return lax.ppermute(array_of, ("yh", "c"), pairs)


def shards(hidden, grad_out, weight):
    z, yh, x, yl, c = (lax.axis_index(name) for name in FINE)
    y = 2 * yh + yl
    low, first = yh == 0, c == 0
    tokens, units = hidden.shape
    half = units // 2
    width = weight.shape[1]
    part = tokens // 3

    xa = jnp.stack(around(grad_out[:part], "x"))
    yb = jnp.stack(around(grad_out[part:], Y))

    w_lo, w_hi = weight[:half], weight[half:]
    w0 = cross(pick(first, w_lo, w_hi), 0, False)
    w1 = cross(pick(first, w_hi, w_lo), 1, False)
    mine = jnp.concatenate([pick(low, w0, w1), pick(low, w1, w0)], axis=0)
    rows = lax.all_gather(mine, "z", axis=0, tiled=True).reshape(8, 2, half, width)

    ht = hidden.T
    keep, send = pick(low, ht[:half], ht[half:]), pick(low, ht[half:], ht[:half])
    got = shift(send, "yh", 1)
    own = jnp.concatenate([pick(low, keep, got), pick(low, got, keep)], axis=1)
    other = shift(own, "c", 1)
    ht = jnp.concatenate([pick(first, own, other), pick(first, other, own)], axis=0)

    ga = jnp.stack(around(xa, Y))
    gb = jnp.stack(around(yb, "x"))

    def slots(owner):
        owner = owner % 8
        xs = slot(owner // 2 - x + 4)
        ys = [slot(2 * k + owner % 2 - y + 4) for k in range(2)]
        return jnp.stack([xs] + ys, axis=-1).reshape(-1).astype(jnp.int32)

    near = jnp.array([4, 3, 5], jnp.int32)
    rest = jnp.array([2, 6, 1, 7, 0], jnp.int32)
    t1 = terms(ht, ga, gb, slots(z + near))
    t = {4: t1[0], 3: t1[1], 5: t1[2]}

    def message(a, b):
        return jnp.concatenate([encode(a), encode(b)], axis=0)

    size = half + EXTRA
    right = shift(message(t[4][:half], t[3][half:]), "z", 1)
    left = shift(message(t[5][:half], t[4][half:]), "z", -1)
    t2 = terms(ht, ga, gb, slots(z + rest))
    for i, r in enumerate((2, 6, 1, 7, 0)):
        t[r] = t2[i]

    for step in (2, 3):
        new = []
        for got, a, b in ((right, 5 - step, 4 - step), (left, 4 + step, 3 + step)):
            new.append(
                message(
                    decode(got[:size]) + t[a][:half], decode(got[size:]) + t[b][half:]
                )
            )
        right, left = shift(new[0], "z", 1), shift(new[1], "z", -1)
    right4 = shift(encode(decode(right[:size]) + t[1][:half]), "z", 1)
    left4 = shift(encode(decode(left[size:]) + t[7][half:]), "z", -1)
    gw_a = (decode(right4) + decode(left[:size]) + t[0][:half]).astype(jnp.bfloat16)
    gw_b = (decode(right[size:]) + decode(left4) + t[0][half:]).astype(jnp.bfloat16)

    q0 = cross(pick(low, gw_a, gw_b), 0, True)
    q1 = cross(pick(low, gw_b, gw_a), 1, True)
    grad_weight = jnp.concatenate([pick(first, q0, q1), pick(first, q1, q0)], axis=0)

    everyone = slots(jnp.arange(8, dtype=jnp.int32))
    row_block = lambda b: jnp.concatenate([everyone, b.reshape(1).astype(jnp.int32)])
    gh_other = shift(hidden_part(ga, gb, rows, row_block(1 - c)), "c", 1)
    gh = (hidden_part(ga, gb, rows, row_block(c)) + gh_other).astype(jnp.bfloat16)
    gh_keep, gh_send = pick(low, gh[0], gh[1]), pick(low, gh[1], gh[0])
    gh_got = shift(gh_send, "yh", 1)
    grad_hidden = jnp.concatenate(
        [pick(low, gh_keep, gh_got), pick(low, gh_got, gh_keep)], axis=1
    )
    return (grad_hidden, grad_weight)


def solution(mesh):
    fine = Mesh(mesh.devices.reshape(8, 2, 4, 2, 2), FINE)
    dp, tensor = FINE[:2], FINE[2:]
    return jax.shard_map(
        shards,
        mesh=fine,
        in_specs=(P(dp, tensor), P(dp, tensor), P(tensor, dp)),
        out_specs=(P(dp, tensor), P(tensor, dp)),
        check_vma=False,
    )
```

```python
import functools

import jax
import jax.numpy as jnp
from jax import lax
from jax.experimental import pallas as pl
from jax.experimental.pallas import tpu as pltpu
from jax.sharding import Mesh, PartitionSpec as P

FINE = ("z", "yh", "x", "yl", "c")
SIZE = {"z": 8, "x": 4, ("yh", "yl"): 4, "yh": 2, "c": 2}
Y = ("yh", "yl")
Z = 8
EXTRA = 16
SPREAD = 2.0**7.875
MIB = 2**20
F32 = jnp.float32
BF16 = jnp.bfloat16


def shift(array, axis, by):
    size = SIZE[axis]
    return lax.ppermute(array, axis, [(i, (i + by) % size) for i in range(size)])


def swap(array, axis, by):
    return lax.ppermute(array, axis, [(i, i ^ by) for i in range(SIZE[axis])])


def pick(first, a, b):
    return jnp.where(first, a, b)


def tie(values, *after):
    return lax.optimization_barrier((values, after))[0]


def params(mib):
    return pltpu.CompilerParams(vmem_limit_bytes=mib * MIB)


def cost(flops, size):
    return pl.CostEstimate(flops=flops, bytes_accessed=size, transcendentals=0)


def decode(code, e):
    code = code.astype(F32)
    root = lax.rsqrt(lax.rsqrt(lax.rsqrt(lax.rsqrt(jnp.abs(code)))))
    return jnp.where(code < 0, -root, root) * (jnp.exp2(e.astype(F32)) * (1 / SPREAD))


def decode_ref(ref, i, rows):
    return decode(ref[i, :rows], ref[i, rows : rows + 1])


def encode_ref(ref, i, total):
    rows = total.shape[0]
    top = jnp.max(jnp.abs(total), axis=0, keepdims=True)
    e = jnp.ceil(jnp.log2(jnp.maximum(top, 1e-30)))
    u = total * (jnp.exp2(-e) * SPREAD)
    u2 = u * u
    u4 = u2 * u2
    u8 = u4 * u4
    u16 = u8 * u8
    ref[i, :rows] = jnp.where(total < 0, -u16, u16).astype(BF16)
    ref[i, rows:] = jnp.broadcast_to(e, (EXTRA, total.shape[1])).astype(BF16)


def term_spec(term, owner, half):
    rows = term.shape[1] // 2
    return pl.BlockSpec((1, rows, term.shape[2]), lambda i: (owner % Z, half, 0))


def whole(array):
    return pl.BlockSpec(array.shape, lambda i, n=array.ndim: (0,) * n)


def message(term, parts, got=None, first=0):
    rows, width = term.shape[1] // 2, term.shape[2]
    n = len(parts)

    def kernel(*refs):
        out = refs[-1]
        for i in range(n):
            total = refs[i][0]
            if got is not None:
                total = total + decode_ref(refs[n], first + i, rows)
            encode_ref(out, i, total)

    args = [term] * n + ([] if got is None else [got])
    shape = (n, rows + EXTRA, width)
    return pl.pallas_call(
        kernel,
        out_shape=jax.ShapeDtypeStruct(shape, BF16),
        grid=(1,),
        in_specs=[term_spec(term, *part) for part in parts]
        + ([] if got is None else [whole(got)]),
        out_specs=pl.BlockSpec(shape, lambda i: (0, 0, 0)),
        compiler_params=params(16),
        cost_estimate=cost(n * rows * width * 30, n * rows * width * 8),
    )(*args)


def last(term, right, right4, left, left4, swapped):
    rows, width = term.shape[1] // 2, term.shape[2]

    def kernel(s, ta, tb, r3, r4, l3, l4, o0, o1):
        a = decode_ref(r4, 0, rows) + decode_ref(l3, 0, rows) + ta[0]
        b = decode_ref(r3, 1, rows) + decode_ref(l4, 0, rows) + tb[0]
        flip = s[0] == 1
        a, b = a.astype(BF16), b.astype(BF16)

        @pl.when(flip)
        def _():
            o0[...] = b
            o1[...] = a

        @pl.when(jnp.logical_not(flip))
        def _():
            o0[...] = a
            o1[...] = b

    spec = lambda shape: pl.BlockSpec(shape, lambda i, s, n=len(shape): (0,) * n)
    out = jax.ShapeDtypeStruct((rows, width), BF16)
    return pl.pallas_call(
        kernel,
        out_shape=(out, out),
        grid_spec=pltpu.PrefetchScalarGridSpec(
            num_scalar_prefetch=1,
            grid=(1,),
            in_specs=[
                pl.BlockSpec((1, rows, width), lambda i, s: (0, 0, 0)),
                pl.BlockSpec((1, rows, width), lambda i, s: (0, 1, 0)),
                spec(right.shape),
                spec(right4.shape),
                spec(left.shape),
                spec(left4.shape),
            ],
            out_specs=[spec(out.shape), spec(out.shape)],
        ),
        compiler_params=params(16),
        cost_estimate=cost(rows * width * 60, rows * width * 24),
    )(swapped, term, term, right, right4, left, left4)


def terms(buffer, ht, ga, gb, xs, places):
    rows = ht.shape[0]
    ta, tb = ga.shape[1], gb.shape[0]
    width = gb.shape[1] // 2

    def kernel(s, *refs):
        ht_ref, own, pair, b, out = refs[-5:]
        a = jnp.concatenate([own[0], pair[0]], axis=0)
        out[0] = jnp.dot(
            ht_ref[:, : 2 * ta], a, preferred_element_type=F32
        ) + jnp.dot(ht_ref[:, 2 * ta :], b[...], preferred_element_type=F32)

    first = [] if buffer is None else [buffer]
    return pl.pallas_call(
        kernel,
        out_shape=jax.ShapeDtypeStruct((Z, rows, width), F32),
        grid_spec=pltpu.PrefetchScalarGridSpec(
            num_scalar_prefetch=1,
            grid=(2,),
            in_specs=[pl.BlockSpec(memory_space=pl.ANY) for _ in first]
            + [
                pl.BlockSpec(ht.shape, lambda i, s: (0, 0)),
                pl.BlockSpec((1, ta, width), lambda i, s: (i, 0, xs)),
                pl.BlockSpec((1, ta, width), lambda i, s: (2 + i, 0, xs)),
                pl.BlockSpec((tb, width), lambda i, s: (0, i)),
            ],
            out_specs=pl.BlockSpec((1, rows, width), lambda i, s: (s[i], 0, 0)),
        ),
        input_output_aliases={} if buffer is None else {1: 0},
        compiler_params=params(24),
        cost_estimate=cost(
            4 * rows * width * ht.shape[1], 2 * rows * width * 4 + ht.size * 2 + gb.size * 2
        ),
    )(places, *first, ht, ga, ga, gb)


def hidden_part(ga, gbs, weights, where, got, lanes):
    half, width = weights.shape[2:]
    tile = ga.shape[1]
    per = gbs[0].shape[0] // tile // 2
    n = 1 + per
    deep = Z * width
    dims = (((1,), (1,)), ((), ()))

    def kernel(s, a_ref, *refs):
        b_refs, w_refs = refs[:4], refs[4 : 4 + 2 * Z]
        if got is None:
            out, wa, wb = refs[4 + 2 * Z :]
        else:
            got_ref, own, pair, wa, wb = refs[4 + 2 * Z :]
        i = pl.program_id(0)

        @pl.when(i == 0)
        def _():
            for k in range(Z):
                wa[:, k * width : (k + 1) * width] = w_refs[k][0, 0]
                wb[:, k * width : (k + 1) * width] = w_refs[Z + k][0, 0]

        def finish(part):
            if got is None:
                out[:, :half] = part
                out[:, half:] = jnp.zeros((tile, lanes - half), F32)
                return
            part = (part + got_ref[:, :half]).astype(BF16)

            @pl.when(i < n)
            def _():
                own[:, :half] = part
                own[:, half:] = jnp.zeros((tile, lanes - half), BF16)

            @pl.when(i >= n)
            def _():
                pair[:, :half] = part
                pair[:, half:] = jnp.zeros((tile, lanes - half), BF16)

        @pl.when(i % n == 0)
        def _():
            g = jnp.concatenate([a_ref[0], a_ref[1]], axis=1)
            finish(lax.dot_general(g, wa[...], dims, preferred_element_type=F32))

        @pl.when(i % n != 0)
        def _():
            g = jnp.concatenate([b[...] for b in b_refs], axis=1)
            finish(lax.dot_general(g, wb[...], dims, preferred_element_type=F32))

    row = lambda i, s: (per * (i // n) + jnp.maximum(i % n - 1, 0), 0)
    w_spec = lambda k: pl.BlockSpec(
        (1, 1, half, width), lambda i, s: (s[k], s[2 * Z], 0, 0)
    )
    tokens = 2 * n * tile
    if got is None:
        out_shape = jax.ShapeDtypeStruct((tokens, lanes), F32)
        out_specs = pl.BlockSpec((tile, lanes), lambda i, s: (i, 0))
    else:
        out_shape = (jax.ShapeDtypeStruct((n * tile, lanes), BF16),) * 2
        out_specs = [
            pl.BlockSpec((tile, lanes), lambda i, s: (jnp.minimum(i, n - 1), 0)),
            pl.BlockSpec((tile, lanes), lambda i, s: (jnp.maximum(i - n, 0), 0)),
        ]
    extra = [] if got is None else [pl.BlockSpec((tile, lanes), lambda i, s: (i, 0))]
    return pl.pallas_call(
        kernel,
        out_shape=out_shape,
        grid_spec=pltpu.PrefetchScalarGridSpec(
            num_scalar_prefetch=1,
            grid=(2 * n,),
            in_specs=[pl.BlockSpec((2, tile, ga.shape[2]), lambda i, s: (i // n, 0, 0))]
            + [pl.BlockSpec((tile, gbs[0].shape[1]), row)] * 4
            + [w_spec(k) for k in range(2 * Z)]
            + extra,
            out_specs=out_specs,
            scratch_shapes=[pltpu.VMEM((half, deep), BF16)] * 2,
        ),
        compiler_params=params(32),
        cost_estimate=cost(2 * tokens * deep * half, 2 * tokens * deep + 4 * tokens * lanes),
    )(where, ga, *gbs, *[weights] * (2 * Z), *([] if got is None else [got]))


def cross(array, k, out):
    pairs = []
    for p in range(2):
        for q in range(2):
            to = (q, p ^ k) if out else (q ^ k, p)
            pairs.append((p * 2 + q, to[0] * 2 + to[1]))
    return lax.ppermute(array, ("yh", "c"), pairs)


def far(near, axis):
    one, three = near
    cut = one.shape[0] // 2
    top = swap(one[:cut], axis, 3)
    bottom = swap(three[cut:], axis, 1)
    return jnp.concatenate([top, bottom], axis=0)


def shards(hidden, grad_out, weight):
    z, yh, x, yl, c = (lax.axis_index(name) for name in FINE)
    low, first = yh == 0, c == 0
    tokens, units = hidden.shape
    half = units // 2
    width = weight.shape[1]
    part = tokens // 3

    a, b = grad_out[:part], grad_out[part:]
    b1, b3, b2 = swap(b, Y, 1), swap(b, Y, 3), swap(b, Y, 2)
    a1, a3, a2 = swap(a, "x", 1), swap(a, "x", 3), swap(a, "x", 2)
    gb0 = jnp.concatenate(
        [jnp.concatenate([b, b1], axis=1), jnp.concatenate([b2, b3], axis=1)], axis=0
    )
    ga0 = jnp.concatenate([a, a1, a2, a3], axis=1)
    gb1, gb3 = swap(gb0, "x", 1), swap(gb0, "x", 3)
    ga1, ga3 = swap(ga0, Y, 1), swap(ga0, Y, 3)
    gb2 = far((gb1, gb3), "x")
    ga2 = far((ga1, ga3), Y)
    ga = jnp.stack([ga0, ga1, ga2, ga3])
    gbs = [gb0, gb1, gb2, gb3]

    ht = hidden.T
    keep, send = pick(low, ht[:half], ht[half:]), pick(low, ht[half:], ht[:half])
    got = swap(tie(send, b2), "yh", 1)
    own = jnp.concatenate(
        [keep[:, :part], got[:, :part], keep[:, part:], got[:, part:]], axis=1
    )
    other = swap(own, "c", 1)
    ht = jnp.concatenate([pick(first, own, other), pick(first, other, own)], axis=0)

    w_lo, w_hi = weight[:half], weight[half:]
    w0 = cross(tie(pick(first, w_lo, w_hi), b2), 0, False)
    w1 = cross(tie(pick(first, w_hi, w_lo), b2), 1, False)
    mine = jnp.concatenate([pick(low, w0, w1), pick(low, w1, w0)], axis=0)
    rows = lax.all_gather(mine, "z", axis=0, tiled=True).reshape(Z, 2, half, width)

    me = 2 * x + yl

    def places(xs):
        owner = me ^ jnp.array([2 * xs, 2 * xs + 1], jnp.int32)
        return ((owner - z + Z) % Z).astype(jnp.int32)

    term = None
    for xs in (0, 1, 3, 2):
        term = terms(term, ht, ga, gbs[xs], xs, places(xs))

    right = shift(message(term, [(4, 0), (3, 1)]), "z", 1)
    left = shift(message(term, [(5, 0), (4, 1)]), "z", -1)

    order_a = [2 * xs + ys for ys in range(2) for xs in range(4)]
    order_b = list(range(Z))
    owners = me ^ jnp.array(order_a + order_b, jnp.int32)
    where = lambda block: jnp.concatenate([owners, block.reshape(1)]).astype(jnp.int32)
    lanes = -(-half // 128) * 128
    gh_other = swap(hidden_part(ga, gbs, rows, where(1 - c), None, lanes), "c", 1)

    for step in (2, 3):
        right = message(term, [(5 - step, 0), (4 - step, 1)], right)
        left = message(term, [(4 + step, 0), (3 + step, 1)], left)
        right, left = shift(right, "z", 1), shift(left, "z", -1)
    right4 = shift(message(term, [(1, 0)], right, 0), "z", 1)
    left4 = shift(message(term, [(7, 1)], left, 1), "z", -1)

    gh_keep, gh_send = hidden_part(ga, gbs, rows, where(c), gh_other, lanes)
    gh_got = swap(gh_send, "yh", 1)
    gh_keep, gh_got = gh_keep[:, :half], gh_got[:, :half]
    grad_hidden = jnp.concatenate(
        [pick(low, gh_keep, gh_got), pick(low, gh_got, gh_keep)], axis=1
    )

    q0, q1 = last(term, right, right4, left, left4, yh.reshape(1).astype(jnp.int32))
    q0, q1 = cross(q0, 0, True), cross(q1, 1, True)
    grad_weight = jnp.concatenate([pick(first, q0, q1), pick(first, q1, q0)], axis=0)
    return (grad_hidden, grad_weight)


def solution(mesh):
    fine = Mesh(mesh.devices.reshape(Z, 2, 4, 2, 2), FINE)
    dp, tensor = FINE[:2], FINE[2:]
    return jax.shard_map(
        shards,
        mesh=fine,
        in_specs=(P(dp, tensor), P(dp, tensor), P(tensor, dp)),
        out_specs=(P(dp, tensor), P(tensor, dp)),
        check_vma=False,
    )
```

```python
import functools

import jax
import jax.numpy as jnp
from jax import lax
from jax.experimental import pallas as pl
from jax.experimental.pallas import tpu as pltpu
from jax.sharding import Mesh, PartitionSpec as P

FINE = ("z", "yh", "x", "yl", "c")
SIZE = {"z": 8, "x": 4, ("yh", "yl"): 4, "yh": 2, "c": 2}
Y = ("yh", "yl")
Z = 8
EXTRA = 16
SPREAD = 2.0**7.875
MIB = 2**20
F32 = jnp.float32
BF16 = jnp.bfloat16


def shift(array, axis, by):
    size = SIZE[axis]
    return lax.ppermute(array, axis, [(i, (i + by) % size) for i in range(size)])


def swap(array, axis, by):
    return lax.ppermute(array, axis, [(i, i ^ by) for i in range(SIZE[axis])])


def pick(first, a, b):
    return jnp.where(first, a, b)


def tie(values, *after):
    return lax.optimization_barrier((values, after))[0]


def params(mib):
    return pltpu.CompilerParams(vmem_limit_bytes=mib * MIB)


def cost(flops, size):
    return pl.CostEstimate(flops=flops, bytes_accessed=size, transcendentals=0)


def decode(code, e):
    code = code.astype(F32)
    root = lax.rsqrt(lax.rsqrt(lax.rsqrt(lax.rsqrt(jnp.abs(code)))))
    return jnp.where(code < 0, -root, root) * (jnp.exp2(e.astype(F32)) * (1 / SPREAD))


def decode_ref(ref, i, rows):
    return decode(ref[i, :rows], ref[i, rows : rows + 1])


def encode_ref(ref, i, total):
    rows = total.shape[0]
    top = jnp.max(jnp.abs(total), axis=0, keepdims=True)
    e = jnp.ceil(jnp.log2(jnp.maximum(top, 1e-30)))
    u = total * (jnp.exp2(-e) * SPREAD)
    u2 = u * u
    u4 = u2 * u2
    u8 = u4 * u4
    u16 = u8 * u8
    ref[i, :rows] = jnp.where(total < 0, -u16, u16).astype(BF16)
    ref[i, rows:] = jnp.broadcast_to(e, (EXTRA, total.shape[1])).astype(BF16)


def term_spec(term, owner, half):
    rows = term.shape[1] // 2
    return pl.BlockSpec((1, rows, term.shape[2]), lambda i: (owner % Z, half, 0))


def whole(array):
    return pl.BlockSpec(array.shape, lambda i, n=array.ndim: (0,) * n)


def message(term, parts, got=None, first=0):
    rows, width = term.shape[1] // 2, term.shape[2]
    n = len(parts)

    def kernel(*refs):
        out = refs[-1]
        for i in range(n):
            total = refs[i][0]
            if got is not None:
                total = total + decode_ref(refs[n], first + i, rows)
            encode_ref(out, i, total)

    args = [term] * n + ([] if got is None else [got])
    shape = (n, rows + EXTRA, width)
    return pl.pallas_call(
        kernel,
        out_shape=jax.ShapeDtypeStruct(shape, BF16),
        grid=(1,),
        in_specs=[term_spec(term, *part) for part in parts]
        + ([] if got is None else [whole(got)]),
        out_specs=pl.BlockSpec(shape, lambda i: (0, 0, 0)),
        compiler_params=params(16),
        cost_estimate=cost(n * rows * width * 30, n * rows * width * 8),
    )(*args)


def last(term, right, right4, left, left4, swapped):
    rows, width = term.shape[1] // 2, term.shape[2]

    def kernel(s, ta, tb, r3, r4, l3, l4, o0, o1):
        a = decode_ref(r4, 0, rows) + decode_ref(l3, 0, rows) + ta[0]
        b = decode_ref(r3, 1, rows) + decode_ref(l4, 0, rows) + tb[0]
        flip = s[0] == 1
        a, b = a.astype(BF16), b.astype(BF16)

        @pl.when(flip)
        def _():
            o0[...] = b
            o1[...] = a

        @pl.when(jnp.logical_not(flip))
        def _():
            o0[...] = a
            o1[...] = b

    spec = lambda shape: pl.BlockSpec(shape, lambda i, s, n=len(shape): (0,) * n)
    out = jax.ShapeDtypeStruct((rows, width), BF16)
    return pl.pallas_call(
        kernel,
        out_shape=(out, out),
        grid_spec=pltpu.PrefetchScalarGridSpec(
            num_scalar_prefetch=1,
            grid=(1,),
            in_specs=[
                pl.BlockSpec((1, rows, width), lambda i, s: (0, 0, 0)),
                pl.BlockSpec((1, rows, width), lambda i, s: (0, 1, 0)),
                spec(right.shape),
                spec(right4.shape),
                spec(left.shape),
                spec(left4.shape),
            ],
            out_specs=[spec(out.shape), spec(out.shape)],
        ),
        compiler_params=params(16),
        cost_estimate=cost(rows * width * 60, rows * width * 24),
    )(swapped, term, term, right, right4, left, left4)


def terms(buffer, ht, ga, gb, xs, places):
    rows = ht.shape[0]
    ta, tb = ga.shape[1], gb[0].shape[0]
    width = gb[0].shape[1] // 2

    def kernel(s, *refs):
        ht_ref, a0, a1, b0, b1, out = refs[-6:]
        g = jnp.concatenate([a0[0], a1[0], b0[...], b1[...]], axis=0)
        out[0] = jnp.dot(ht_ref[...], g, preferred_element_type=F32)

    first = [] if buffer is None else [buffer]
    return pl.pallas_call(
        kernel,
        out_shape=jax.ShapeDtypeStruct((Z, rows, width), F32),
        grid_spec=pltpu.PrefetchScalarGridSpec(
            num_scalar_prefetch=1,
            grid=(2,),
            in_specs=[pl.BlockSpec(memory_space=pl.ANY) for _ in first]
            + [
                pl.BlockSpec(ht.shape, lambda i, s: (0, 0)),
                pl.BlockSpec((1, ta, width), lambda i, s: (i, 0, xs)),
                pl.BlockSpec((1, ta, width), lambda i, s: (2 + i, 0, xs)),
                pl.BlockSpec((tb, width), lambda i, s: (0, i)),
                pl.BlockSpec((tb, width), lambda i, s: (0, i)),
            ],
            out_specs=pl.BlockSpec((1, rows, width), lambda i, s: (s[i], 0, 0)),
        ),
        input_output_aliases={} if buffer is None else {1: 0},
        compiler_params=params(24),
        cost_estimate=cost(
            4 * rows * width * ht.shape[1], 2 * rows * width * 4 + ht.size * 2 + tb * width * 8
        ),
    )(places, *first, ht, ga, ga, *gb)


def hidden_part(ga, gbs, weights, where, got, lanes):
    half, width = weights.shape[2:]
    tile = ga.shape[1]
    gbs = [block for gb in gbs for block in gb]
    per = gbs[0].shape[0] // tile
    n = 1 + per
    deep = Z * width
    dims = (((1,), (1,)), ((), ()))

    def kernel(s, a_ref, *refs):
        b_refs, w_refs = refs[:8], refs[8 : 8 + 2 * Z]
        if got is None:
            out, wa, wb = refs[8 + 2 * Z :]
        else:
            got_ref, own, pair, wa, wb = refs[8 + 2 * Z :]
        i = pl.program_id(0)

        @pl.when(i == 0)
        def _():
            for k in range(Z):
                wa[:, k * width : (k + 1) * width] = w_refs[k][0, 0]
                wb[:, k * width : (k + 1) * width] = w_refs[Z + k][0, 0]

        def finish(part):
            if got is None:
                out[:, :half] = part
                out[:, half:] = jnp.zeros((tile, lanes - half), F32)
                return
            part = (part + got_ref[:, :half]).astype(BF16)

            @pl.when(i < n)
            def _():
                own[:, :half] = part
                own[:, half:] = jnp.zeros((tile, lanes - half), BF16)

            @pl.when(i >= n)
            def _():
                pair[:, :half] = part
                pair[:, half:] = jnp.zeros((tile, lanes - half), BF16)

        @pl.when(i % n == 0)
        def _():
            g = jnp.concatenate([a_ref[0], a_ref[1]], axis=1)
            finish(lax.dot_general(g, wa[...], dims, preferred_element_type=F32))

        for block in range(2):

            @pl.when(jnp.logical_and(i % n != 0, i // n == block))
            def _():
                g = jnp.concatenate([b[...] for b in b_refs[block::2]], axis=1)
                finish(lax.dot_general(g, wb[...], dims, preferred_element_type=F32))

    own_row = lambda i, s: (jnp.clip(i - 1, 0, per - 1), 0)
    pair_row = lambda i, s: (jnp.clip(i - n - 1, 0, per - 1), 0)
    w_spec = lambda k: pl.BlockSpec(
        (1, 1, half, width), lambda i, s: (s[k], s[2 * Z], 0, 0)
    )
    tokens = 2 * n * tile
    if got is None:
        out_shape = jax.ShapeDtypeStruct((tokens, lanes), F32)
        out_specs = pl.BlockSpec((tile, lanes), lambda i, s: (i, 0))
    else:
        out_shape = (jax.ShapeDtypeStruct((n * tile, lanes), BF16),) * 2
        out_specs = [
            pl.BlockSpec((tile, lanes), lambda i, s: (jnp.minimum(i, n - 1), 0)),
            pl.BlockSpec((tile, lanes), lambda i, s: (jnp.maximum(i - n, 0), 0)),
        ]
    extra = [] if got is None else [pl.BlockSpec((tile, lanes), lambda i, s: (i, 0))]
    return pl.pallas_call(
        kernel,
        out_shape=out_shape,
        grid_spec=pltpu.PrefetchScalarGridSpec(
            num_scalar_prefetch=1,
            grid=(2 * n,),
            in_specs=[pl.BlockSpec((2, tile, ga.shape[2]), lambda i, s: (i // n, 0, 0))]
            + [
                pl.BlockSpec((tile, gbs[0].shape[1]), row)
                for row in (own_row, pair_row) * 4
            ]
            + [w_spec(k) for k in range(2 * Z)]
            + extra,
            out_specs=out_specs,
            scratch_shapes=[pltpu.VMEM((half, deep), BF16)] * 2,
        ),
        compiler_params=params(56),
        cost_estimate=cost(2 * tokens * deep * half, 2 * tokens * deep + 4 * tokens * lanes),
    )(where, ga, *gbs, *[weights] * (2 * Z), *([] if got is None else [got]))


def cross(array, k, out):
    pairs = []
    for p in range(2):
        for q in range(2):
            to = (q, p ^ k) if out else (q ^ k, p)
            pairs.append((p * 2 + q, to[0] * 2 + to[1]))
    return lax.ppermute(array, ("yh", "c"), pairs)


def shards(hidden, grad_out, weight):
    z, yh, x, yl, c = (lax.axis_index(name) for name in FINE)
    low, first = yh == 0, c == 0
    tokens, units = hidden.shape
    half = units // 2
    width = weight.shape[1]
    part = tokens // 3

    a, b = grad_out[:part], grad_out[part:]
    b1, b3, b2 = swap(b, Y, 1), swap(b, Y, 3), swap(b, Y, 2)
    a1, a3, a2 = swap(a, "x", 1), swap(a, "x", 3), swap(a, "x", 2)
    own0 = jnp.concatenate([b, b1], axis=1)
    pair0 = jnp.concatenate([b2, b3], axis=1)
    own1, own3 = swap(own0, "x", 1), swap(own0, "x", 3)
    pair1, pair3 = swap(pair0, "x", 1), swap(pair0, "x", 3)
    own2, pair2 = swap(own1, "x", 3), swap(pair3, "x", 1)
    gbs = [(own0, pair0), (own1, pair1), (own2, pair2), (own3, pair3)]

    ht = hidden.T
    keep, send = pick(low, ht[:half], ht[half:]), pick(low, ht[half:], ht[:half])
    got = swap(tie(send, own0, pair0), "yh", 1)

    ga0 = tie(jnp.concatenate([a, a1, a2, a3], axis=1), own0, pair0)
    ga1, ga3, ga2 = swap(ga0, Y, 1), swap(ga0, Y, 3), swap(ga0, Y, 2)
    ga = jnp.stack([ga0, ga1, ga2, ga3])

    own = jnp.concatenate(
        [keep[:, :part], got[:, :part], keep[:, part:], got[:, part:]], axis=1
    )
    other = swap(own, "c", 1)
    ht = jnp.concatenate([pick(first, own, other), pick(first, other, own)], axis=0)

    weight = tie(weight, own1, own3)
    w_lo, w_hi = weight[:half], weight[half:]
    w0 = cross(pick(first, w_lo, w_hi), 0, False)
    w1 = cross(pick(first, w_hi, w_lo), 1, False)
    mine = jnp.concatenate([pick(low, w0, w1), pick(low, w1, w0)], axis=0)
    rows = lax.all_gather(mine, "z", axis=0, tiled=True).reshape(Z, 2, half, width)

    me = 2 * x + yl

    def places(xs):
        owner = me ^ jnp.array([2 * xs, 2 * xs + 1], jnp.int32)
        return ((owner - z + Z) % Z).astype(jnp.int32)

    term = None
    for xs in (0, 1, 3, 2):
        term = terms(term, ht, ga, gbs[xs], xs, places(xs))

    right = message(term, [(4, 0), (3, 1)])
    left = message(term, [(5, 0), (4, 1)])
    sent = (right, left)
    right, left = shift(right, "z", 1), shift(left, "z", -1)

    order_a = [2 * xs + ys for ys in range(2) for xs in range(4)]
    order_b = list(range(Z))
    owners = me ^ jnp.array(order_a + order_b, jnp.int32)
    where = lambda block: jnp.concatenate([owners, block.reshape(1)]).astype(jnp.int32)
    lanes = -(-half // 128) * 128
    product = hidden_part(ga, gbs, rows, tie(where(1 - c), *sent), None, lanes)
    gh_other = swap(product, "c", 1)

    right, left = tie((right, left), product)
    right = message(term, [(3, 0), (2, 1)], right)
    left = message(term, [(6, 0), (5, 1)], left)
    sent = (right, left)
    right, left = shift(right, "z", 1), shift(left, "z", -1)

    gh_keep, gh_send = hidden_part(
        ga, gbs, rows, tie(where(c), *sent), gh_other, lanes
    )
    gh_got = swap(gh_send, "yh", 1)

    right, left = tie((right, left), gh_send)
    right = message(term, [(2, 0), (1, 1)], right)
    left = message(term, [(7, 0), (6, 1)], left)
    right, left = shift(right, "z", 1), shift(left, "z", -1)
    right4 = shift(message(term, [(1, 0)], right, 0), "z", 1)
    left4 = shift(message(term, [(7, 1)], left, 1), "z", -1)

    gh_keep, gh_got = gh_keep[:, :half], gh_got[:, :half]
    grad_hidden = jnp.concatenate(
        [pick(low, gh_keep, gh_got), pick(low, gh_got, gh_keep)], axis=1
    )

    q0, q1 = last(term, right, right4, left, left4, yh.reshape(1).astype(jnp.int32))
    q0, q1 = cross(q0, 0, True), cross(q1, 1, True)
    grad_weight = jnp.concatenate([pick(first, q0, q1), pick(first, q1, q0)], axis=0)
    return (grad_hidden, grad_weight)


def solution(mesh):
    fine = Mesh(mesh.devices.reshape(Z, 2, 4, 2, 2), FINE)
    dp, tensor = FINE[:2], FINE[2:]
    return jax.shard_map(
        shards,
        mesh=fine,
        in_specs=(P(dp, tensor), P(dp, tensor), P(tensor, dp)),
        out_specs=(P(dp, tensor), P(tensor, dp)),
        check_vma=False,
    )
```

```python
import functools

import jax
import jax.numpy as jnp
from jax import lax
from jax.experimental import pallas as pl
from jax.experimental.pallas import tpu as pltpu
from jax.sharding import Mesh, PartitionSpec as P

FINE = ("z", "yh", "x", "yl", "c")
SIZE = {"z": 8, "x": 4, ("yh", "yl"): 4, "yh": 2, "c": 2}
Y = ("yh", "yl")
Z = 8
EXTRA = 16
SPREAD = 2.0**7.875
MIB = 2**20
F32 = jnp.float32
BF16 = jnp.bfloat16


def shift(array, axis, by):
    size = SIZE[axis]
    return lax.ppermute(array, axis, [(i, (i + by) % size) for i in range(size)])


def swap(array, axis, by):
    return lax.ppermute(array, axis, [(i, i ^ by) for i in range(SIZE[axis])])


def pick(first, a, b):
    return jnp.where(first, a, b)


def tie(values, *after):
    return lax.optimization_barrier((values, after))[0]


def params(mib):
    return pltpu.CompilerParams(vmem_limit_bytes=mib * MIB)


SMALL = pl.CostEstimate(flops=1000, bytes_accessed=1000, transcendentals=0)


def decode(code, e):
    code = code.astype(F32)
    root = lax.rsqrt(lax.rsqrt(lax.rsqrt(lax.rsqrt(jnp.abs(code)))))
    return jnp.where(code < 0, -root, root) * (jnp.exp2(e.astype(F32)) * (1 / SPREAD))


def decode_ref(ref, rows):
    return decode(ref[:rows], ref[rows : rows + 1])


def encode_ref(ref, total):
    rows = total.shape[0]
    top = jnp.max(jnp.abs(total), axis=0, keepdims=True)
    e = jnp.ceil(jnp.log2(jnp.maximum(top, 1e-30)))
    u = total * (jnp.exp2(-e) * SPREAD)
    u2 = u * u
    u4 = u2 * u2
    u8 = u4 * u4
    u16 = u8 * u8
    ref[:rows] = jnp.where(total < 0, -u16, u16).astype(BF16)
    ref[rows:] = jnp.broadcast_to(e, (EXTRA, total.shape[1])).astype(BF16)


PAIRING = (
    [(0, 1), (1, 0), (2, 3), (3, 2), (4, 5), (5, 4), (6, 7), (7, 6)],
    [(1, 2), (2, 1), (3, 4), (4, 3), (5, 6), (6, 5), (7, 0), (0, 7)],
)


def ring_call(kernel, term, picks, got, out_rows, n_out):
    rows, width = term.shape[1] // 2, term.shape[2]
    specs = [
        pl.BlockSpec((1, rows, width), lambda i, at=at: (at[0], at[1], 0))
        for at in picks
    ] + [pl.BlockSpec(g.shape, lambda i: (0, 0)) for g in got]
    out = jax.ShapeDtypeStruct((out_rows, width), BF16)
    return pl.pallas_call(
        kernel,
        out_shape=(out,) * n_out,
        grid=(1,),
        in_specs=specs,
        out_specs=[pl.BlockSpec(out.shape, lambda i: (0, 0))] * n_out,
        compiler_params=params(8),
        cost_estimate=SMALL,
    )(*[term] * len(picks), *got)


def hop(term, slot, half, got):
    rows = term.shape[1] // 2

    def kernel(t, *refs):
        total = t[0]
        if got is not None:
            total = total + decode_ref(refs[0], rows)
        encode_ref(refs[-1], total)

    got_ = [] if got is None else [got]
    return ring_call(kernel, term, [(slot, half)], got_, rows + EXTRA, 1)[0]


def last(term, three, four):
    rows = term.shape[1] // 2

    def kernel(t0, t1, a0, b1, f0, f1, o0, o1):
        o0[...] = (t0[0] + decode_ref(a0, rows) + decode_ref(f1, rows)).astype(BF16)
        o1[...] = (t1[0] + decode_ref(b1, rows) + decode_ref(f0, rows)).astype(BF16)

    got = [three[0][1], three[1][0], *four]
    return ring_call(kernel, term, [(0, 0), (0, 1)], got, rows, 2)


def exchange(array, pairing):
    return lax.ppermute(array, "z", PAIRING[pairing])


def terms(buffer, ht, ga, gb, xs, places):
    rows = ht.shape[0]
    ta, tb = ga.shape[1], gb.shape[0]
    width = gb.shape[1] // 2

    def kernel(s, *refs):
        ht_ref, own, pair, b, out = refs[-5:]
        g = jnp.concatenate([own[0], pair[0], b[...]], axis=0)
        out[0] = jnp.dot(ht_ref[...], g, preferred_element_type=F32)

    first = [] if buffer is None else [buffer]
    return pl.pallas_call(
        kernel,
        out_shape=jax.ShapeDtypeStruct((Z, rows, width), F32),
        grid_spec=pltpu.PrefetchScalarGridSpec(
            num_scalar_prefetch=1,
            grid=(2,),
            in_specs=[pl.BlockSpec(memory_space=pl.ANY) for _ in first]
            + [
                pl.BlockSpec(ht.shape, lambda i, s: (0, 0)),
                pl.BlockSpec((1, ta, width), lambda i, s: (i, 0, xs)),
                pl.BlockSpec((1, ta, width), lambda i, s: (2 + i, 0, xs)),
                pl.BlockSpec((tb, width), lambda i, s: (0, i)),
            ],
            out_specs=pl.BlockSpec((1, rows, width), lambda i, s: (s[i], 0, 0)),
        ),
        input_output_aliases={} if buffer is None else {1: 0},
        compiler_params=params(24),
        cost_estimate=SMALL,
    )(places, *first, ht, ga, ga, gb)


def hidden_product(ga, gbs, weights, where, lanes, block):
    half, width = weights.shape[1], weights.shape[2] // 2
    part = ga[0].shape[1]
    tile = part // 2
    deep = Z * width
    dims = (((1,), (1,)), ((), ()))

    def kernel(s, *refs):
        a_refs, b_refs, w_ref, (out, w) = refs[:2], refs[2:10], refs[10], refs[11:]
        i = pl.program_id(0)

        @pl.when(i == 0)
        def _():
            for core in range(2):
                at = pl.ds(pl.multiple_of((s[Z] ^ core) * width, width), width)
                for k in range(Z):
                    place = core * deep + k * width
                    w[:, place : place + width] = w_ref[s[k], :, at]

        def finish(g):
            total = lax.dot_general(g, w[...], dims, preferred_element_type=F32)
            out[:, :half] = total.astype(BF16)
            out[:, half:] = jnp.zeros((tile, lanes - half), BF16)

        @pl.when(i < 2)
        def _():
            finish(
                jnp.concatenate(
                    [
                        a[ys, :, xs * width : (xs + 1) * width]
                        for a in a_refs
                        for xs in range(4)
                        for ys in range(2)
                    ],
                    axis=1,
                )
            )

        @pl.when(i >= 2)
        def _():
            finish(jnp.concatenate([b[...] for b in b_refs], axis=1))

    a_spec = pl.BlockSpec(
        (2, tile, ga[0].shape[2]), lambda i, s: (block, jnp.minimum(i, 1), 0)
    )
    b_spec = pl.BlockSpec(
        (tile, 2 * width), lambda i, s: (2 * block + jnp.maximum(i - 2, 0), 0)
    )
    return pl.pallas_call(
        kernel,
        out_shape=jax.ShapeDtypeStruct((2 * part, lanes), BF16),
        grid_spec=pltpu.PrefetchScalarGridSpec(
            num_scalar_prefetch=1,
            grid=(4,),
            in_specs=[a_spec] * 2
            + [b_spec] * 8
            + [pl.BlockSpec(weights.shape, lambda i, s: (0, 0, 0))],
            out_specs=pl.BlockSpec((tile, lanes), lambda i, s: (i, 0)),
            scratch_shapes=[pltpu.VMEM((half, 2 * deep), BF16)],
        ),
        compiler_params=params(56),
        cost_estimate=SMALL,
    )(where, *ga, *gbs[0], *gbs[1], weights)


def cross(array, k):
    pairs = [(p * 2 + q, q * 2 + (p ^ k)) for p in range(2) for q in range(2)]
    return lax.ppermute(array, ("yh", "c"), pairs)


def shards(hidden, grad_out, weight):
    z, yh, x, yl, c = (lax.axis_index(name) for name in FINE)
    low, first = yh == 0, c == 0
    tokens, units = hidden.shape
    half = units // 2
    width = weight.shape[1]
    part = tokens // 2

    a, b = grad_out[:part], grad_out[part:]
    b1, b3, b2 = swap(b, Y, 1), swap(b, Y, 3), swap(b, Y, 2)
    a = tie(a, b1)
    a1, a3, a2 = swap(a, "x", 1), swap(a, "x", 3), swap(a, "x", 2)
    ht = hidden.T
    h_keep, send = pick(low, ht[:half], ht[half:]), pick(low, ht[half:], ht[:half])
    h_got = swap(send, "yh", 1)
    w_keep = pick(low, weight[:half], weight[half:])
    w_got = swap(pick(low, weight[half:], weight[:half]), "yh", 1)
    a, a1, a2, a3, b, b1, b2, b3, h_keep, h_got, w_keep, w_got = lax.optimization_barrier(
        (a, a1, a2, a3, b, b1, b2, b3, h_keep, h_got, w_keep, w_got)
    )

    ga0 = jnp.concatenate([a, a1, a2, a3], axis=1)
    gb0 = jnp.concatenate(
        [jnp.concatenate([b, b1], axis=1), jnp.concatenate([b2, b3], axis=1)], axis=0
    )
    gb1, gb3, gb2 = swap(gb0, "x", 1), swap(gb0, "x", 3), swap(gb0, "x", 2)
    ga1, ga3, ga2 = swap(ga0, Y, 1), swap(ga0, Y, 3), swap(ga0, Y, 2)
    h_own = jnp.concatenate(
        [h_keep[:, :part], h_got[:, :part], h_keep[:, part:], h_got[:, part:]], axis=1
    )
    h_other = swap(h_own, "c", 1)
    mine = jnp.concatenate([pick(low, w_keep, w_got), pick(low, w_got, w_keep)], axis=1)
    rows = lax.all_gather(mine, "z", axis=0, tiled=True).reshape(Z, half, 2 * width)
    ga0, ga1, ga2, ga3, gb0, gb1, gb2, gb3, h_own, h_other = lax.optimization_barrier(
        (ga0, ga1, ga2, ga3, gb0, gb1, gb2, gb3, h_own, h_other)
    )
    odd = z % 2 == 1
    straight = first != odd
    ht = jnp.concatenate(
        [pick(straight, h_own, h_other), pick(straight, h_other, h_own)], axis=0
    )
    ga = jnp.stack([ga0, ga1, ga2, ga3])
    gbs = [gb0, gb1, gb2, gb3]

    me = 2 * x + yl

    def places(xs):
        owner = me ^ jnp.array([2 * xs, 2 * xs + 1], jnp.int32)
        return (jnp.where(odd, z - owner, owner - z) + Z).astype(jnp.int32) % Z

    term = None
    for xs in (0, 1, 3, 2):
        term = terms(term, ht, ga, gbs[xs], xs, places(xs))

    ga_other = swap(ga, "c", 1)
    gbs_other = [swap(gb, "c", 1) for gb in gbs]
    owners = me ^ jnp.arange(Z, dtype=jnp.int32)
    where = jnp.concatenate([owners, c.reshape(1)]).astype(jnp.int32)
    lanes = -(-half // 128) * 128

    product = functools.partial(
        hidden_product, (ga, ga_other), (gbs, gbs_other), rows, lanes=lanes
    )

    def step_on(step, got):
        new = [
            [
                hop(term, [5 - step, 4 + step][p] - h, h, got[1 - p][1 - h])
                for h in range(2)
            ]
            for p in range(2)
        ]
        return new, [[exchange(new[p][h], p) for h in range(2)] for p in range(2)]

    new, got = step_on(1, [[None, None], [None, None]])
    gh_send = product(where=tie(where, new), block=1)
    gh_got = swap(gh_send, "yh", 1)
    got = tie(got, gh_send)
    new, got = step_on(2, got)
    gh_keep = product(where=tie(where, new), block=0)
    got = tie(got, gh_keep)
    new, got = step_on(3, got)
    four = [
        exchange(hop(term, 1, 0, got[1][1]), 0),
        exchange(hop(term, 7, 1, got[0][0]), 1),
    ]

    gh_keep, gh_got = gh_keep[:, :half], gh_got[:, :half]
    grad_hidden = jnp.concatenate(
        [pick(low, gh_keep, gh_got), pick(low, gh_got, gh_keep)], axis=1
    )

    q0, q1 = last(term, got, four)
    straight = low != odd
    q0, q1 = pick(straight, q0, q1), pick(straight, q1, q0)
    q0, q1 = cross(q0, 0), cross(q1, 1)
    grad_weight = jnp.concatenate([pick(first, q0, q1), pick(first, q1, q0)], axis=0)
    return (grad_hidden, grad_weight)


def solution(mesh):
    fine = Mesh(mesh.devices.reshape(Z, 2, 4, 2, 2), FINE)
    dp, tensor = FINE[:2], FINE[2:]
    return jax.shard_map(
        shards,
        mesh=fine,
        in_specs=(P(dp, tensor), P(dp, tensor), P(tensor, dp)),
        out_specs=(P(dp, tensor), P(tensor, dp)),
        check_vma=False,
    )
```

```python
import functools

import jax
import jax.numpy as jnp
from jax import lax
from jax.experimental import pallas as pl
from jax.experimental.pallas import tpu as pltpu
from jax.sharding import Mesh, PartitionSpec as P

FINE = ("z", "yh", "x", "yl", "c")
SIZE = {"z": 8, "x": 4, ("yh", "yl"): 4, "yh": 2, "c": 2, ("z", "yh"): 16}
Y = ("yh", "yl")
Z = 8
EXTRA = 16
SPREAD = 2.0**7.875
MIB = 2**20
F32 = jnp.float32
BF16 = jnp.bfloat16


def swap(array, axis, by):
    return lax.ppermute(array, axis, [(i, i ^ by) for i in range(SIZE[axis])])


def pick(first, a, b):
    return jnp.where(first, a, b)


def tie(values, *after):
    return lax.optimization_barrier((values, after))[0]


def params(mib):
    return pltpu.CompilerParams(vmem_limit_bytes=mib * MIB)


SMALL = pl.CostEstimate(flops=1000, bytes_accessed=1000, transcendentals=0)


def decode(code, e):
    code = code.astype(F32)
    root = lax.rsqrt(lax.rsqrt(lax.rsqrt(lax.rsqrt(jnp.abs(code)))))
    return jnp.where(code < 0, -root, root) * (jnp.exp2(e.astype(F32)) * (1 / SPREAD))


def decode_ref(ref, rows):
    return decode(ref[:rows], ref[rows : rows + 1])


def encode_ref(ref, total):
    rows = total.shape[0]
    top = jnp.max(jnp.abs(total), axis=0, keepdims=True)
    e = jnp.ceil(jnp.log2(jnp.maximum(top, 1e-30)))
    u = total * (jnp.exp2(-e) * SPREAD)
    u2 = u * u
    u4 = u2 * u2
    u8 = u4 * u4
    u16 = u8 * u8
    ref[:rows] = jnp.where(total < 0, -u16, u16).astype(BF16)
    ref[rows:] = jnp.broadcast_to(e, (EXTRA, total.shape[1])).astype(BF16)


PAIRING = (
    [(0, 1), (1, 0), (2, 3), (3, 2), (4, 5), (5, 4), (6, 7), (7, 6)],
    [(1, 2), (2, 1), (3, 4), (4, 3), (5, 6), (6, 5), (7, 0), (0, 7)],
)


def ring_call(kernel, term, picks, got, out_rows, n_out):
    rows, width = term.shape[1] // 2, term.shape[2]
    specs = [
        pl.BlockSpec((1, rows, width), lambda i, at=at: (at[0], at[1], 0))
        for at in picks
    ] + [pl.BlockSpec(g.shape, lambda i: (0, 0)) for g in got]
    out = jax.ShapeDtypeStruct((out_rows, width), BF16)
    return pl.pallas_call(
        kernel,
        out_shape=(out,) * n_out,
        grid=(1,),
        in_specs=specs,
        out_specs=[pl.BlockSpec(out.shape, lambda i: (0, 0))] * n_out,
        compiler_params=params(8),
        cost_estimate=SMALL,
    )(*[term] * len(picks), *got)


def hop(term, slot, half, got):
    rows = term.shape[1] // 2

    def kernel(t, *refs):
        total = t[0]
        if got is not None:
            total = total + decode_ref(refs[0], rows)
        encode_ref(refs[-1], total)

    got_ = [] if got is None else [got]
    return ring_call(kernel, term, [(slot, half)], got_, rows + EXTRA, 1)[0]


def last(term, three, four):
    rows = term.shape[1] // 2

    def kernel(t0, t1, a0, b1, f0, f1, o0, o1):
        o0[...] = (t0[0] + decode_ref(a0, rows) + decode_ref(f1, rows)).astype(BF16)
        o1[...] = (t1[0] + decode_ref(b1, rows) + decode_ref(f0, rows)).astype(BF16)

    got = [three[0][1], three[1][0], *four]
    return ring_call(kernel, term, [(0, 0), (0, 1)], got, rows, 2)


def exchange(array, pairing):
    return lax.ppermute(array, "z", PAIRING[pairing])


def terms(buffer, ht, ga, gb, xs, places):
    rows = ht.shape[0]
    ta, tb = ga.shape[1], gb.shape[0]
    width = gb.shape[1] // 2

    def kernel(s, *refs):
        ht_ref, own, pair, b, out = refs[-5:]
        g = jnp.concatenate([own[0], pair[0], b[...]], axis=0)
        out[0] = jnp.dot(ht_ref[...], g, preferred_element_type=F32)

    first = [] if buffer is None else [buffer]
    return pl.pallas_call(
        kernel,
        out_shape=jax.ShapeDtypeStruct((Z, rows, width), F32),
        grid_spec=pltpu.PrefetchScalarGridSpec(
            num_scalar_prefetch=1,
            grid=(2,),
            in_specs=[pl.BlockSpec(memory_space=pl.ANY) for _ in first]
            + [
                pl.BlockSpec(ht.shape, lambda i, s: (0, 0)),
                pl.BlockSpec((1, ta, width), lambda i, s: (i, 0, xs)),
                pl.BlockSpec((1, ta, width), lambda i, s: (2 + i, 0, xs)),
                pl.BlockSpec((tb, width), lambda i, s: (0, i)),
            ],
            out_specs=pl.BlockSpec((1, rows, width), lambda i, s: (s[i], 0, 0)),
        ),
        input_output_aliases={} if buffer is None else {1: 0},
        compiler_params=params(24),
        cost_estimate=SMALL,
    )(places, *first, ht, ga, ga, gb)


def hidden_product(ga, gbs, weights, where, lanes):
    half, width = weights.shape[1:]
    tile = ga[0].shape[1]
    per = gbs[0][0].shape[0] // (2 * tile)
    n = 1 + per
    deep = Z * width
    dims = (((1,), (1,)), ((), ()))

    def kernel(s, *refs):
        a_refs, b_refs, w_refs, (own, pair, w) = refs[:2], refs[2:10], refs[10:18], refs[18:]
        i = pl.program_id(0)

        @pl.when(i == 0)
        def _():
            for core in range(2):
                for k in range(Z):
                    place = core * deep + k * width
                    w[:, place : place + width] = w_refs[k][core]

        def finish(g):
            part = lax.dot_general(g, w[...], dims, preferred_element_type=F32)
            part = part.astype(BF16)
            for out, mine in ((own, i < n), (pair, i >= n)):

                @pl.when(mine)
                def _():
                    out[:, :half] = part
                    out[:, half:] = jnp.zeros((tile, lanes - half), BF16)

        @pl.when(i % n == 0)
        def _():
            finish(
                jnp.concatenate(
                    [
                        a[ys, :, xs * width : (xs + 1) * width]
                        for a in a_refs
                        for xs in range(4)
                        for ys in range(2)
                    ],
                    axis=1,
                )
            )

        @pl.when(i % n != 0)
        def _():
            finish(jnp.concatenate([b[...] for b in b_refs], axis=1))

    out = jax.ShapeDtypeStruct((n * tile, lanes), BF16)
    a_spec = pl.BlockSpec((2, tile, ga[0].shape[2]), lambda i, s: (i // n, 0, 0))
    b_spec = pl.BlockSpec(
        (tile, 2 * width), lambda i, s: (per * (i // n) + jnp.maximum(i % n - 1, 0), 0)
    )
    return pl.pallas_call(
        kernel,
        out_shape=(out, out),
        grid_spec=pltpu.PrefetchScalarGridSpec(
            num_scalar_prefetch=1,
            grid=(2 * n,),
            in_specs=[a_spec] * 2
            + [b_spec] * 8
            + [
                pl.BlockSpec((2, half, width), lambda i, s, k=k: (s[k], 0, 0))
                for k in range(Z)
            ],
            out_specs=[
                pl.BlockSpec((tile, lanes), lambda i, s: (jnp.minimum(i, n - 1), 0)),
                pl.BlockSpec((tile, lanes), lambda i, s: (jnp.maximum(i - n, 0), 0)),
            ],
            scratch_shapes=[pltpu.VMEM((half, 2 * deep), BF16)],
        ),
        compiler_params=params(50),
        cost_estimate=SMALL,
    )(where, *ga, *gbs[0], *gbs[1], *[weights] * Z)


def cross(array, k):
    pairs = [(p * 2 + q, q * 2 + (p ^ k)) for p in range(2) for q in range(2)]
    return lax.ppermute(array, ("yh", "c"), pairs)


def shards(hidden, grad_out, weight):
    z, yh, x, yl, c = (lax.axis_index(name) for name in FINE)
    low, first = yh == 0, c == 0
    tokens, units = hidden.shape
    half = units // 2
    width = weight.shape[1]
    part = tokens // 3
    odd = z % 2 == 1

    a, b = grad_out[:part], grad_out[part:]
    b1, b3, b2 = swap(b, Y, 1), swap(b, Y, 3), swap(b, Y, 2)
    a1, a3, a2 = swap(a, "x", 1), swap(a, "x", 3), swap(a, "x", 2)
    w_keep = pick(low, weight[:half], weight[half:])
    w_send = pick(low, weight[half:], weight[:half])
    w_pair, w_near = swap(w_send, "yh", 1), swap(w_keep, "z", 1)
    w_cross = swap(w_send, ("z", "yh"), 3)
    ht = hidden.T
    h_keep, h_send = pick(low, ht[:half], ht[half:]), pick(low, ht[half:], ht[:half])
    a, a1, a2, a3, b, b1, b2, b3, h_keep, h_send, w_keep, w_pair, w_near, w_cross = (
        lax.optimization_barrier(
            (a, a1, a2, a3, b, b1, b2, b3, h_keep, h_send, w_keep, w_pair, w_near, w_cross)
        )
    )

    ga0 = jnp.concatenate([a, a1, a2, a3], axis=1)
    gb0 = jnp.concatenate(
        [jnp.concatenate([b, b1], axis=1), jnp.concatenate([b2, b3], axis=1)], axis=0
    )
    gb1, gb3 = swap(gb0, "x", 1), swap(gb0, "x", 3)
    ga1 = swap(ga0, Y, 1)
    h_got = swap(h_send, "yh", 1)
    same = yh == c
    by_core = lambda t, u: [pick(same, t, u), pick(same, u, t)]
    here, there = by_core(w_keep, w_pair), by_core(w_near, w_cross)
    w0 = jnp.stack(
        [pick(odd, t, u) for t, u in zip(there, here)]
        + [pick(odd, t, u) for t, u in zip(here, there)]
    )
    w1 = exchange(w0, 1)
    ga0, ga1, gb0, gb1, gb3, h_keep, h_got, w0, w1 = lax.optimization_barrier(
        (ga0, ga1, gb0, gb1, gb3, h_keep, h_got, w0, w1)
    )

    gb2 = swap(gb0, "x", 2)
    ga3, ga2 = swap(ga0, Y, 3), swap(ga0, Y, 2)
    h_own = jnp.concatenate(
        [h_keep[:, :part], h_got[:, :part], h_keep[:, part:], h_got[:, part:]], axis=1
    )
    h_other = swap(h_own, "c", 1)
    w2 = exchange(w1, 0)
    ga0, ga1, ga2, ga3, gb0, gb1, gb2, gb3, h_own, h_other, w0, w1, w2 = (
        lax.optimization_barrier(
            (ga0, ga1, ga2, ga3, gb0, gb1, gb2, gb3, h_own, h_other, w0, w1, w2)
        )
    )

    w3 = exchange(w2, 1)
    rows = jnp.concatenate([w0, w1, w2, w3], axis=0)
    straight = first != odd
    ht = jnp.concatenate(
        [pick(straight, h_own, h_other), pick(straight, h_other, h_own)], axis=0
    )
    ga = jnp.stack([ga0, ga1, ga2, ga3])
    gbs = [gb0, gb1, gb2, gb3]

    me = 2 * x + yl

    def places(xs):
        owner = me ^ jnp.array([2 * xs, 2 * xs + 1], jnp.int32)
        return (jnp.where(odd, z - owner, owner - z) + Z).astype(jnp.int32) % Z

    term = None
    for xs in (0, 1, 3, 2):
        term = terms(term, ht, ga, gbs[xs], xs, places(xs))

    ga_other = swap(ga, "c", 1)
    gbs_other = [swap(gb, "c", 1) for gb in gbs]
    owners = me ^ jnp.arange(Z, dtype=jnp.int32)
    off = (owners // 2 - z // 2 + 4) % 4
    held = jnp.where(
        off == 0, 0, jnp.where(off == 2, 3, jnp.where((off == 1) == odd, 1, 2))
    )
    where = (2 * held + owners % 2).astype(jnp.int32)
    lanes = -(-half // 128) * 128

    def step_on(step, got):
        new = [
            [
                hop(term, [5 - step, 4 + step][p] - h, h, got[1 - p][1 - h])
                for h in range(2)
            ]
            for p in range(2)
        ]
        return new, [[exchange(new[p][h], p) for h in range(2)] for p in range(2)]

    _, got = step_on(1, [[None, None], [None, None]])
    new, got = step_on(2, got)
    gh_keep, gh_send = hidden_product(
        (ga, ga_other), (gbs, gbs_other), rows, tie(where, new), lanes
    )
    gh_got = swap(gh_send, "yh", 1)
    _, got = step_on(3, tie(got, gh_send))
    four = [
        exchange(hop(term, 1, 0, got[1][1]), 0),
        exchange(hop(term, 7, 1, got[0][0]), 1),
    ]

    gh_keep, gh_got = gh_keep[:, :half], gh_got[:, :half]
    grad_hidden = jnp.concatenate(
        [pick(low, gh_keep, gh_got), pick(low, gh_got, gh_keep)], axis=1
    )

    q0, q1 = last(term, got, four)
    straight = low != odd
    q0, q1 = pick(straight, q0, q1), pick(straight, q1, q0)
    q0, q1 = cross(q0, 0), cross(q1, 1)
    grad_weight = jnp.concatenate([pick(first, q0, q1), pick(first, q1, q0)], axis=0)
    return (grad_hidden, grad_weight)


def solution(mesh):
    fine = Mesh(mesh.devices.reshape(Z, 2, 4, 2, 2), FINE)
    dp, tensor = FINE[:2], FINE[2:]
    return jax.shard_map(
        shards,
        mesh=fine,
        in_specs=(P(dp, tensor), P(dp, tensor), P(tensor, dp)),
        out_specs=(P(dp, tensor), P(tensor, dp)),
        check_vma=False,
    )
```

```python
import functools

import jax
import jax.numpy as jnp
from jax import lax
from jax.experimental import pallas as pl
from jax.experimental.pallas import tpu as pltpu
from jax.sharding import Mesh, PartitionSpec as P

FINE = ("z", "yh", "x", "yl", "c")
SIZE = {"z": 8, "x": 4, ("yh", "yl"): 4, "yh": 2, "c": 2, ("z", "yh"): 16}
Y = ("yh", "yl")
Z = 8
EXTRA = 16
SPREAD = 2.0**7.875
MIB = 2**20
F32 = jnp.float32
BF16 = jnp.bfloat16


def swap(array, axis, by):
    return lax.ppermute(array, axis, [(i, i ^ by) for i in range(SIZE[axis])])


def pick(first, a, b):
    return jnp.where(first, a, b)


def tie(values, *after):
    return lax.optimization_barrier((values, after))[0]


def params(mib):
    return pltpu.CompilerParams(vmem_limit_bytes=mib * MIB)


SMALL = pl.CostEstimate(flops=1000, bytes_accessed=1000, transcendentals=0)


def decode(code, e):
    code = code.astype(F32)
    root = lax.rsqrt(lax.rsqrt(lax.rsqrt(lax.rsqrt(jnp.abs(code)))))
    return jnp.where(code < 0, -root, root) * (jnp.exp2(e.astype(F32)) * (1 / SPREAD))


def decode_ref(ref, rows):
    return decode(ref[:rows], ref[rows : rows + 1])


def encode_ref(ref, total):
    rows = total.shape[0]
    top = jnp.max(jnp.abs(total), axis=0, keepdims=True)
    e = jnp.ceil(jnp.log2(jnp.maximum(top, 1e-30)))
    u = total * (jnp.exp2(-e) * SPREAD)
    u2 = u * u
    u4 = u2 * u2
    u8 = u4 * u4
    u16 = u8 * u8
    ref[:rows] = jnp.where(total < 0, -u16, u16).astype(BF16)
    ref[rows:] = jnp.broadcast_to(e, (EXTRA, total.shape[1])).astype(BF16)


PAIRING = (
    [(0, 1), (1, 0), (2, 3), (3, 2), (4, 5), (5, 4), (6, 7), (7, 6)],
    [(1, 2), (2, 1), (3, 4), (4, 3), (5, 6), (6, 5), (7, 0), (0, 7)],
)


def ring_call(kernel, term, picks, got, out_rows, n_out):
    rows, width = term.shape[1] // 2, term.shape[2]
    specs = [
        pl.BlockSpec((1, rows, width), lambda i, at=at: (at[0], at[1], 0))
        for at in picks
    ] + [pl.BlockSpec(g.shape, lambda i: (0, 0)) for g in got]
    out = jax.ShapeDtypeStruct((out_rows, width), BF16)
    return pl.pallas_call(
        kernel,
        out_shape=(out,) * n_out,
        grid=(1,),
        in_specs=specs,
        out_specs=[pl.BlockSpec(out.shape, lambda i: (0, 0))] * n_out,
        compiler_params=params(8),
        cost_estimate=SMALL,
    )(*[term] * len(picks), *got)


def hop(term, slot, half, got):
    rows = term.shape[1] // 2

    def kernel(t, *refs):
        total = t[0]
        if got is not None:
            total = total + decode_ref(refs[0], rows)
        encode_ref(refs[-1], total)

    got_ = [] if got is None else [got]
    return ring_call(kernel, term, [(slot, half)], got_, rows + EXTRA, 1)[0]


def last(term, three, four):
    rows = term.shape[1] // 2

    def kernel(t0, t1, a0, b1, f0, f1, o0, o1):
        o0[...] = (t0[0] + decode_ref(a0, rows) + decode_ref(f1, rows)).astype(BF16)
        o1[...] = (t1[0] + decode_ref(b1, rows) + decode_ref(f0, rows)).astype(BF16)

    got = [three[0][1], three[1][0], *four]
    return ring_call(kernel, term, [(0, 0), (0, 1)], got, rows, 2)


def exchange(array, pairing):
    return lax.ppermute(array, "z", PAIRING[pairing])


def terms(buffer, ht, ga, gb, xs, places):
    rows = ht.shape[0]
    ta, tb = ga.shape[1], gb.shape[0]
    width = gb.shape[1] // 2

    def kernel(s, *refs):
        ht_ref, own, pair, b, out = refs[-5:]
        g = jnp.concatenate([own[0], pair[0], b[...]], axis=0)
        out[0] = jnp.dot(ht_ref[...], g, preferred_element_type=F32)

    first = [] if buffer is None else [buffer]
    return pl.pallas_call(
        kernel,
        out_shape=jax.ShapeDtypeStruct((Z, rows, width), F32),
        grid_spec=pltpu.PrefetchScalarGridSpec(
            num_scalar_prefetch=1,
            grid=(2,),
            in_specs=[pl.BlockSpec(memory_space=pl.ANY) for _ in first]
            + [
                pl.BlockSpec(ht.shape, lambda i, s: (0, 0)),
                pl.BlockSpec((1, ta, width), lambda i, s: (i, 0, xs)),
                pl.BlockSpec((1, ta, width), lambda i, s: (2 + i, 0, xs)),
                pl.BlockSpec((tb, width), lambda i, s: (0, i)),
            ],
            out_specs=pl.BlockSpec((1, rows, width), lambda i, s: (s[i], 0, 0)),
        ),
        input_output_aliases={} if buffer is None else {1: 0},
        compiler_params=params(24),
        cost_estimate=SMALL,
    )(places, *first, ht, ga, ga, gb)


def hidden_product(ga, gbs, weights, where, lanes, block):
    half, width = weights.shape[1:]
    ta, tb = ga[0].shape[1], gbs[0][0].shape[0] // 2
    deep = Z * width
    dims = (((1,), (1,)), ((), ()))

    def kernel(s, *refs):
        a_refs, b_refs, w_ref, (out, g, w, sems) = refs[:2], refs[2:10], refs[10], refs[11:]
        early, late = [], []

        def fetch(group, src, dst):
            copy = pltpu.make_async_copy(src, dst, sems.at[len(early) + len(late)])
            copy.start()
            group.append(copy)

        for core in range(2):
            for k in range(Z):
                place = pl.ds(core * deep + k * width, width)
                fetch(early, w_ref.at[2 * s[k] + core], w.at[:, place])
                src = a_refs[core].at[2 * block + k % 2, :, pl.ds(k // 2 * width, width)]
                fetch(early, src, g.at[pl.ds(0, ta), place])
        for core in range(2):
            for k in range(Z // 2):
                place = pl.ds(core * deep + k * 2 * width, 2 * width)
                src = b_refs[core * 4 + k].at[pl.ds(block * tb, tb)]
                fetch(late, src, g.at[pl.ds(ta, tb), place])
        out[:, half:] = jnp.zeros((ta + tb, lanes - half), BF16)
        for group, rows in ((early, slice(0, ta)), (late, slice(ta, ta + tb))):
            for copy in group:
                copy.wait()
            out[rows, :half] = lax.dot_general(
                g[rows], w[...], dims, preferred_element_type=F32
            ).astype(BF16)

    hbm = pl.BlockSpec(memory_space=pltpu.HBM)
    return pl.pallas_call(
        kernel,
        out_shape=jax.ShapeDtypeStruct((ta + tb, lanes), BF16),
        in_specs=[pl.BlockSpec(memory_space=pltpu.SMEM)] + [hbm] * 11,
        out_specs=pl.BlockSpec(memory_space=pltpu.VMEM),
        scratch_shapes=[
            pltpu.VMEM((ta + tb, 2 * deep), BF16),
            pltpu.VMEM((half, 2 * deep), BF16),
            pltpu.SemaphoreType.DMA((5 * Z,)),
        ],
        compiler_params=params(24),
        cost_estimate=SMALL,
    )(where, *ga, *gbs[0], *gbs[1], weights)


def cross(array, k):
    pairs = [(p * 2 + q, q * 2 + (p ^ k)) for p in range(2) for q in range(2)]
    return lax.ppermute(array, ("yh", "c"), pairs)


def shards(hidden, grad_out, weight):
    z, yh, x, yl, c = (lax.axis_index(name) for name in FINE)
    low, first = yh == 0, c == 0
    tokens, units = hidden.shape
    half = units // 2
    width = weight.shape[1]
    part = tokens // 3
    odd = z % 2 == 1

    a, b = grad_out[:part], grad_out[part:]
    b1, b3 = swap(b, Y, 1), swap(b, Y, 3)
    w_keep = pick(low, weight[:half], weight[half:])
    w_send = pick(low, weight[half:], weight[:half])
    b2 = swap(jnp.concatenate([b, w_send], axis=0), Y, 2)
    b2, w_pair = b2[: tokens - part], b2[tokens - part :]
    a1, a3, a2 = swap(a, "x", 1), swap(a, "x", 3), swap(a, "x", 2)
    ht = hidden.T
    h_keep, h_send = pick(low, ht[:half], ht[half:]), pick(low, ht[half:], ht[:half])
    h_got = swap(h_send, "yh", 1)
    a, a1, a2, a3, b, b1, b2, b3, h_keep, h_got, w_keep, w_pair = (
        lax.optimization_barrier(
            (a, a1, a2, a3, b, b1, b2, b3, h_keep, h_got, w_keep, w_pair)
        )
    )

    ga0 = jnp.concatenate([a, a1, a2, a3], axis=1)
    gb0 = jnp.concatenate(
        [jnp.concatenate([b, b1], axis=1), jnp.concatenate([b2, b3], axis=1)], axis=0
    )
    gb1, gb3 = swap(gb0, "x", 1), swap(gb0, "x", 3)
    ga1, ga3, ga2 = swap(ga0, Y, 1), swap(ga0, Y, 3), swap(ga0, Y, 2)
    h_own = jnp.concatenate(
        [h_keep[:, :part], h_got[:, :part], h_keep[:, part:], h_got[:, part:]], axis=1
    )
    h_other = swap(h_own, "c", 1)
    same = yh == c
    mine = jnp.stack([pick(same, w_keep, w_pair), pick(same, w_pair, w_keep)])
    rows = lax.all_gather(mine, "z", axis=0, tiled=True)
    ga0, ga1, ga2, ga3, gb0, gb1, gb3, h_own, h_other = lax.optimization_barrier(
        (ga0, ga1, ga2, ga3, gb0, gb1, gb3, h_own, h_other)
    )

    gb2 = swap(gb0, "x", 2)
    straight = first != odd
    ht = jnp.concatenate(
        [pick(straight, h_own, h_other), pick(straight, h_other, h_own)], axis=0
    )
    ga = jnp.stack([ga0, ga1, ga2, ga3])
    gbs = [gb0, gb1, gb2, gb3]

    me = 2 * x + yl

    def places(xs):
        owner = me ^ jnp.array([2 * xs, 2 * xs + 1], jnp.int32)
        return (jnp.where(odd, z - owner, owner - z) + Z).astype(jnp.int32) % Z

    term = None
    for xs in (0, 1, 3, 2):
        term = terms(term, ht, ga, gbs[xs], xs, places(xs))

    ga_other = swap(ga, "c", 1)
    gbs_other = [swap(gb, "c", 1) for gb in gbs]
    owners = me ^ jnp.arange(Z, dtype=jnp.int32)
    lanes = -(-half // 128) * 128

    def step_on(step, got):
        new = [
            [
                hop(term, [5 - step, 4 + step][p] - h, h, got[1 - p][1 - h])
                for h in range(2)
            ]
            for p in range(2)
        ]
        return new, [[exchange(new[p][h], p) for h in range(2)] for p in range(2)]

    product = functools.partial(
        hidden_product, (ga, ga_other), (gbs, gbs_other), rows, lanes=lanes
    )
    _, got = step_on(1, [[None, None], [None, None]])
    new, got = step_on(2, got)
    gh_send = product(where=tie(owners, new), block=1)
    gh_got = swap(gh_send, "yh", 1)
    new, got = step_on(3, tie(got, gh_send))
    gh_keep = product(where=tie(owners, new), block=0)
    got = tie(got, gh_keep)
    four = [
        exchange(hop(term, 1, 0, got[1][1]), 0),
        exchange(hop(term, 7, 1, got[0][0]), 1),
    ]

    gh_keep, gh_got = gh_keep[:, :half], gh_got[:, :half]
    grad_hidden = jnp.concatenate(
        [pick(low, gh_keep, gh_got), pick(low, gh_got, gh_keep)], axis=1
    )

    q0, q1 = last(term, got, four)
    straight = low != odd
    q0, q1 = pick(straight, q0, q1), pick(straight, q1, q0)
    q0, q1 = cross(q0, 0), cross(q1, 1)
    grad_weight = jnp.concatenate([pick(first, q0, q1), pick(first, q1, q0)], axis=0)
    return (grad_hidden, grad_weight)


def solution(mesh):
    fine = Mesh(mesh.devices.reshape(Z, 2, 4, 2, 2), FINE)
    dp, tensor = FINE[:2], FINE[2:]
    return jax.shard_map(
        shards,
        mesh=fine,
        in_specs=(P(dp, tensor), P(dp, tensor), P(tensor, dp)),
        out_specs=(P(dp, tensor), P(tensor, dp)),
        check_vma=False,
    )
```

```python
import functools

import jax
import jax.numpy as jnp
from jax import lax
from jax.experimental import pallas as pl
from jax.experimental.pallas import tpu as pltpu
from jax.sharding import Mesh, PartitionSpec as P

FINE = ("z", "yh", "x", "yl", "c")
SIZE = {"z": 8, "x": 4, ("yh", "yl"): 4, "yh": 2, "c": 2, ("z", "yh"): 16}
Y = ("yh", "yl")
Z = 8
EXTRA = 16
SPREAD = 2.0**7.875
MIB = 2**20
F32 = jnp.float32
BF16 = jnp.bfloat16


def swap(array, axis, by):
    return lax.ppermute(array, axis, [(i, i ^ by) for i in range(SIZE[axis])])


def pick(first, a, b):
    return jnp.where(first, a, b)


def tie(values, *after):
    return lax.optimization_barrier((values, after))[0]


def params(mib):
    return pltpu.CompilerParams(vmem_limit_bytes=mib * MIB)


SMALL = pl.CostEstimate(flops=1000, bytes_accessed=1000, transcendentals=0)


def decode(code, e):
    code = code.astype(F32)
    root = lax.rsqrt(lax.rsqrt(lax.rsqrt(lax.rsqrt(jnp.abs(code)))))
    return jnp.where(code < 0, -root, root) * (jnp.exp2(e.astype(F32)) * (1 / SPREAD))


def decode_ref(ref, rows):
    return decode(ref[:rows], ref[rows : rows + 1])


def encode_ref(ref, total):
    rows = total.shape[0]
    top = jnp.max(jnp.abs(total), axis=0, keepdims=True)
    e = jnp.ceil(jnp.log2(jnp.maximum(top, 1e-30)))
    u = total * (jnp.exp2(-e) * SPREAD)
    u2 = u * u
    u4 = u2 * u2
    u8 = u4 * u4
    u16 = u8 * u8
    ref[:rows] = jnp.where(total < 0, -u16, u16).astype(BF16)
    ref[rows:] = jnp.broadcast_to(e, (EXTRA, total.shape[1])).astype(BF16)


PAIRING = (
    [(0, 1), (1, 0), (2, 3), (3, 2), (4, 5), (5, 4), (6, 7), (7, 6)],
    [(1, 2), (2, 1), (3, 4), (4, 3), (5, 6), (6, 5), (7, 0), (0, 7)],
)


def ring_call(kernel, term, picks, got, out_rows, n_out):
    rows, width = term.shape[1] // 2, term.shape[2]
    specs = [
        pl.BlockSpec((1, rows, width), lambda i, at=at: (at[0], at[1], 0))
        for at in picks
    ] + [pl.BlockSpec(g.shape, lambda i: (0, 0)) for g in got]
    out = jax.ShapeDtypeStruct((out_rows, width), BF16)
    return pl.pallas_call(
        kernel,
        out_shape=(out,) * n_out,
        grid=(1,),
        in_specs=specs,
        out_specs=[pl.BlockSpec(out.shape, lambda i: (0, 0))] * n_out,
        compiler_params=params(8),
        cost_estimate=SMALL,
    )(*[term] * len(picks), *got)


def hop(term, slot, half, got):
    rows = term.shape[1] // 2

    def kernel(t, *refs):
        total = t[0]
        if got is not None:
            total = total + decode_ref(refs[0], rows)
        encode_ref(refs[-1], total)

    got_ = [] if got is None else [got]
    return ring_call(kernel, term, [(slot, half)], got_, rows + EXTRA, 1)[0]


def last(term, three, four):
    rows = term.shape[1] // 2

    def kernel(t0, t1, a0, b1, f0, f1, o0, o1):
        o0[...] = (t0[0] + decode_ref(a0, rows) + decode_ref(f1, rows)).astype(BF16)
        o1[...] = (t1[0] + decode_ref(b1, rows) + decode_ref(f0, rows)).astype(BF16)

    got = [three[0][1], three[1][0], *four]
    return ring_call(kernel, term, [(0, 0), (0, 1)], got, rows, 2)


def exchange(array, pairing):
    return lax.ppermute(array, "z", PAIRING[pairing])


def terms(buffer, ht, ga, gb, xs, places):
    rows = ht.shape[0]
    ta, tb = ga.shape[1], gb.shape[0]
    width = gb.shape[1] // 2

    def kernel(s, *refs):
        ht_ref, own, pair, b, out = refs[-5:]
        g = jnp.concatenate([own[0], pair[0], b[...]], axis=0)
        out[0] = jnp.dot(ht_ref[...], g, preferred_element_type=F32)

    first = [] if buffer is None else [buffer]
    return pl.pallas_call(
        kernel,
        out_shape=jax.ShapeDtypeStruct((Z, rows, width), F32),
        grid_spec=pltpu.PrefetchScalarGridSpec(
            num_scalar_prefetch=1,
            grid=(2,),
            in_specs=[pl.BlockSpec(memory_space=pl.ANY) for _ in first]
            + [
                pl.BlockSpec(ht.shape, lambda i, s: (0, 0)),
                pl.BlockSpec((1, ta, width), lambda i, s: (i, 0, xs)),
                pl.BlockSpec((1, ta, width), lambda i, s: (2 + i, 0, xs)),
                pl.BlockSpec((tb, width), lambda i, s: (0, i)),
            ],
            out_specs=pl.BlockSpec((1, rows, width), lambda i, s: (s[i], 0, 0)),
        ),
        input_output_aliases={} if buffer is None else {1: 0},
        compiler_params=params(24),
        cost_estimate=SMALL,
    )(places, *first, ht, ga, ga, gb)


def hidden_product(ga, gbs, weights, where, lanes, block):
    half, width = weights.shape[1:]
    ta, tb = ga[0].shape[1], gbs[0][0].shape[0] // 2
    deep = Z * width
    dims = (((1,), (1,)), ((), ()))

    def kernel(s, *refs):
        a_refs, b_refs, w_ref, (out, g, w, sems) = refs[:2], refs[2:10], refs[10], refs[11:]
        early, late = [], []

        def fetch(group, src, dst):
            copy = pltpu.make_async_copy(src, dst, sems.at[len(early) + len(late)])
            copy.start()
            group.append(copy)

        for core in range(2):
            for k in range(Z):
                place = pl.ds(core * deep + k * width, width)
                fetch(early, w_ref.at[2 * s[k] + core], w.at[:, place])
                src = a_refs[core].at[2 * block + k % 2, :, pl.ds(k // 2 * width, width)]
                fetch(early, src, g.at[pl.ds(0, ta), place])
        for core in range(2):
            for k in range(Z // 2):
                place = pl.ds(core * deep + k * 2 * width, 2 * width)
                src = b_refs[core * 4 + k].at[pl.ds(block * tb, tb)]
                fetch(late, src, g.at[pl.ds(ta, tb), place])
        out[:, half:] = jnp.zeros((ta + tb, lanes - half), BF16)
        for group, rows in ((early, slice(0, ta)), (late, slice(ta, ta + tb))):
            for copy in group:
                copy.wait()
            out[rows, :half] = lax.dot_general(
                g[rows], w[...], dims, preferred_element_type=F32
            ).astype(BF16)

    there = pl.BlockSpec(memory_space=pl.ANY)
    return pl.pallas_call(
        kernel,
        out_shape=jax.ShapeDtypeStruct((ta + tb, lanes), BF16),
        in_specs=[pl.BlockSpec(memory_space=pltpu.SMEM)] + [there] * 11,
        out_specs=pl.BlockSpec(memory_space=pltpu.VMEM),
        scratch_shapes=[
            pltpu.VMEM((ta + tb, 2 * deep), BF16),
            pltpu.VMEM((half, 2 * deep), BF16),
            pltpu.SemaphoreType.DMA((5 * Z,)),
        ],
        compiler_params=params(60),
        cost_estimate=SMALL,
    )(where, *ga, *gbs[0], *gbs[1], weights)


def cross(array, k):
    pairs = [(p * 2 + q, q * 2 + (p ^ k)) for p in range(2) for q in range(2)]
    return lax.ppermute(array, ("yh", "c"), pairs)


def shards(hidden, grad_out, weight):
    z, yh, x, yl, c = (lax.axis_index(name) for name in FINE)
    low, first = yh == 0, c == 0
    tokens, units = hidden.shape
    half = units // 2
    width = weight.shape[1]
    part = tokens // 3
    odd = z % 2 == 1

    a, b = grad_out[:part], grad_out[part:]
    b1, b3 = swap(b, Y, 1), swap(b, Y, 3)
    w_keep = pick(low, weight[:half], weight[half:])
    w_send = pick(low, weight[half:], weight[:half])
    b2 = swap(jnp.concatenate([b, w_send], axis=0), Y, 2)
    b2, w_pair = b2[: tokens - part], b2[tokens - part :]
    a1, a3, a2 = swap(a, "x", 1), swap(a, "x", 3), swap(a, "x", 2)
    ht = hidden.T
    h_keep, h_send = pick(low, ht[:half], ht[half:]), pick(low, ht[half:], ht[:half])
    a, a1, a2, a3, b, b1, b2, b3, h_keep, h_send, w_keep, w_pair = (
        lax.optimization_barrier(
            (a, a1, a2, a3, b, b1, b2, b3, h_keep, h_send, w_keep, w_pair)
        )
    )

    ga0 = jnp.concatenate([a, a1, a2, a3], axis=1)
    gb0 = jnp.concatenate(
        [jnp.concatenate([b, b1], axis=1), jnp.concatenate([b2, b3], axis=1)], axis=0
    )
    gb1, gb3 = swap(gb0, "x", 1), swap(gb0, "x", 3)
    ga1, ga3 = swap(ga0, Y, 1), swap(ga0, Y, 3)
    h_got = swap(h_send, "yh", 1)
    same = yh == c
    mine = jnp.stack([pick(same, w_keep, w_pair), pick(same, w_pair, w_keep)])
    rows = lax.all_gather(mine, "z", axis=0, tiled=True)
    ga0, ga1, ga3, gb0, gb1, gb3, h_keep, h_got = lax.optimization_barrier(
        (ga0, ga1, ga3, gb0, gb1, gb3, h_keep, h_got)
    )

    gb2 = swap(gb0, "x", 2)
    ga2 = swap(ga0, Y, 2)
    h_own = jnp.concatenate(
        [h_keep[:, :part], h_got[:, :part], h_keep[:, part:], h_got[:, part:]], axis=1
    )
    h_other = swap(h_own, "c", 1)
    straight = first != odd
    ht = jnp.concatenate(
        [pick(straight, h_own, h_other), pick(straight, h_other, h_own)], axis=0
    )
    ga = jnp.stack([ga0, ga1, ga2, ga3])
    gbs = [gb0, gb1, gb2, gb3]

    me = 2 * x + yl

    def places(xs):
        owner = me ^ jnp.array([2 * xs, 2 * xs + 1], jnp.int32)
        return (jnp.where(odd, z - owner, owner - z) + Z).astype(jnp.int32) % Z

    term = None
    for xs in (0, 1, 3, 2):
        term = terms(term, ht, ga, gbs[xs], xs, places(xs))

    ga_other = swap(ga, "c", 1)
    gbs_other = [swap(gb, "c", 1) for gb in gbs]
    owners = me ^ jnp.arange(Z, dtype=jnp.int32)
    lanes = -(-half // 128) * 128

    def step_on(step, got):
        new = [
            [
                hop(term, [5 - step, 4 + step][p] - h, h, got[1 - p][1 - h])
                for h in range(2)
            ]
            for p in range(2)
        ]
        return new, [[exchange(new[p][h], p) for h in range(2)] for p in range(2)]

    product = functools.partial(
        hidden_product, (ga, ga_other), (gbs, gbs_other), rows, lanes=lanes
    )
    _, got = step_on(1, [[None, None], [None, None]])
    _, got = step_on(2, got)
    new, got = step_on(3, got)
    gh_send = product(where=tie(owners, new), block=1)
    got = tie(got, gh_send)
    sent = [hop(term, 1, 0, got[1][1]), hop(term, 7, 1, got[0][0])]
    four = [exchange(sent[p], p) for p in range(2)]
    gh_got = swap(gh_send, "yh", 1)

    q0, q1 = last(term, got, four)
    straight = low != odd
    q0, q1 = pick(straight, q0, q1), pick(straight, q1, q0)
    gh_keep = product(where=tie(owners, q0, q1), block=0)
    q0, q1 = cross(q0, 0), cross(q1, 1)
    grad_weight = jnp.concatenate([pick(first, q0, q1), pick(first, q1, q0)], axis=0)

    gh_keep, gh_got = gh_keep[:, :half], gh_got[:, :half]
    grad_hidden = jnp.concatenate(
        [pick(low, gh_keep, gh_got), pick(low, gh_got, gh_keep)], axis=1
    )

    return (grad_hidden, grad_weight)


def solution(mesh):
    fine = Mesh(mesh.devices.reshape(Z, 2, 4, 2, 2), FINE)
    dp, tensor = FINE[:2], FINE[2:]
    return jax.shard_map(
        shards,
        mesh=fine,
        in_specs=(P(dp, tensor), P(dp, tensor), P(tensor, dp)),
        out_specs=(P(dp, tensor), P(tensor, dp)),
        check_vma=False,
    )
```

```python
import functools

import jax
import jax.numpy as jnp
from jax import lax
from jax.experimental import pallas as pl
from jax.experimental.pallas import tpu as pltpu
from jax.sharding import Mesh, PartitionSpec as P

FINE = ("z", "yh", "x", "yl", "c")
SIZE = {"z": 8, "x": 4, ("yh", "yl"): 4, "yh": 2, "c": 2, ("z", "yh"): 16}
Y = ("yh", "yl")
Z = 8
EXTRA = 16
SPREAD = 2.0**7.875
MIB = 2**20
F32 = jnp.float32
BF16 = jnp.bfloat16


def swap(array, axis, by):
    return lax.ppermute(array, axis, [(i, i ^ by) for i in range(SIZE[axis])])


def pick(first, a, b):
    return jnp.where(first, a, b)


def tie(values, *after):
    return lax.optimization_barrier((values, after))[0]


def params(mib):
    return pltpu.CompilerParams(vmem_limit_bytes=mib * MIB)


SMALL = pl.CostEstimate(flops=1000, bytes_accessed=1000, transcendentals=0)


def decode(code, e):
    code = code.astype(F32)
    root = lax.rsqrt(lax.rsqrt(lax.rsqrt(lax.rsqrt(jnp.abs(code)))))
    return jnp.where(code < 0, -root, root) * (jnp.exp2(e.astype(F32)) * (1 / SPREAD))


def decode_ref(ref, rows):
    return decode(ref[:rows], ref[rows : rows + 1])


def encode_ref(ref, total):
    rows = total.shape[0]
    top = jnp.max(jnp.abs(total), axis=0, keepdims=True)
    e = jnp.ceil(jnp.log2(jnp.maximum(top, 1e-30)))
    u = total * (jnp.exp2(-e) * SPREAD)
    u2 = u * u
    u4 = u2 * u2
    u8 = u4 * u4
    u16 = u8 * u8
    ref[:rows] = jnp.where(total < 0, -u16, u16).astype(BF16)
    ref[rows:] = jnp.broadcast_to(e, (EXTRA, total.shape[1])).astype(BF16)


PAIRING = (
    [(0, 1), (1, 0), (2, 3), (3, 2), (4, 5), (5, 4), (6, 7), (7, 6)],
    [(1, 2), (2, 1), (3, 4), (4, 3), (5, 6), (6, 5), (7, 0), (0, 7)],
)


def ring_call(kernel, term, picks, got, out_rows, n_out):
    rows, width = term.shape[1] // 2, term.shape[2]
    specs = [
        pl.BlockSpec((1, rows, width), lambda i, at=at: (at[0], at[1], 0))
        for at in picks
    ] + [pl.BlockSpec(g.shape, lambda i: (0, 0)) for g in got]
    out = jax.ShapeDtypeStruct((out_rows, width), BF16)
    return pl.pallas_call(
        kernel,
        out_shape=(out,) * n_out,
        grid=(1,),
        in_specs=specs,
        out_specs=[pl.BlockSpec(out.shape, lambda i: (0, 0))] * n_out,
        compiler_params=params(8),
        cost_estimate=SMALL,
    )(*[term] * len(picks), *got)


def hop(term, slot, half, got):
    rows = term.shape[1] // 2

    def kernel(t, *refs):
        total = t[0]
        if got is not None:
            total = total + decode_ref(refs[0], rows)
        encode_ref(refs[-1], total)

    got_ = [] if got is None else [got]
    return ring_call(kernel, term, [(slot, half)], got_, rows + EXTRA, 1)[0]


def last(term, three, four):
    rows = term.shape[1] // 2

    def kernel(t0, t1, a0, b1, f0, f1, o0, o1):
        o0[...] = (t0[0] + decode_ref(a0, rows) + decode_ref(f1, rows)).astype(BF16)
        o1[...] = (t1[0] + decode_ref(b1, rows) + decode_ref(f0, rows)).astype(BF16)

    got = [three[0][1], three[1][0], *four]
    return ring_call(kernel, term, [(0, 0), (0, 1)], got, rows, 2)


def exchange(array, pairing):
    return lax.ppermute(array, "z", PAIRING[pairing])


def terms(buffer, ht, ga, gb, xs, places):
    rows = ht.shape[0]
    gb = gb if isinstance(gb, tuple) else (gb,)
    ta, width = ga.shape[1], gb[0].shape[1] // 2

    def kernel(s, *refs):
        ht_ref, own, pair, *b, out = refs[len(first) :]
        g = jnp.concatenate([own[0], pair[0]] + [part[...] for part in b], axis=0)
        out[0] = jnp.dot(ht_ref[...], g, preferred_element_type=F32)

    first = [] if buffer is None else [buffer]
    return pl.pallas_call(
        kernel,
        out_shape=jax.ShapeDtypeStruct((Z, rows, width), F32),
        grid_spec=pltpu.PrefetchScalarGridSpec(
            num_scalar_prefetch=1,
            grid=(2,),
            in_specs=[pl.BlockSpec(memory_space=pl.ANY) for _ in first]
            + [
                pl.BlockSpec(ht.shape, lambda i, s: (0, 0)),
                pl.BlockSpec((1, ta, width), lambda i, s: (i, 0, xs)),
                pl.BlockSpec((1, ta, width), lambda i, s: (2 + i, 0, xs)),
            ]
            + [pl.BlockSpec((b.shape[0], width), lambda i, s: (0, i)) for b in gb],
            out_specs=pl.BlockSpec((1, rows, width), lambda i, s: (s[i], 0, 0)),
        ),
        input_output_aliases={} if buffer is None else {1: 0},
        compiler_params=params(24),
        cost_estimate=SMALL,
    )(places, *first, ht, ga, ga, *gb)


def hidden_product(ga, gbs, weights, where, lanes, block):
    half, width = weights.shape[1:]
    ta, tb = ga[0].shape[1], gbs[0][0].shape[0] // 2
    gbs = [[g[block] if isinstance(g, tuple) else g for g in core] for core in gbs]
    deep = Z * width
    dims = (((1,), (1,)), ((), ()))

    def kernel(s, *refs):
        a_refs, b_refs, w_ref, (out, g, w, sems) = refs[:2], refs[2:10], refs[10], refs[11:]
        early, late = [], []

        def fetch(group, src, dst):
            copy = pltpu.make_async_copy(src, dst, sems.at[len(early) + len(late)])
            copy.start()
            group.append(copy)

        for core in range(2):
            for k in range(Z):
                place = pl.ds(core * deep + k * width, width)
                fetch(early, w_ref.at[2 * s[k] + core], w.at[:, place])
                src = a_refs[core].at[2 * block + k % 2, :, pl.ds(k // 2 * width, width)]
                fetch(early, src, g.at[pl.ds(0, ta), place])
        for core in range(2):
            for k in range(Z // 2):
                place = pl.ds(core * deep + k * 2 * width, 2 * width)
                src = b_refs[core * 4 + k]
                if src.shape[0] > tb:
                    src = src.at[pl.ds(block * tb, tb)]
                fetch(late, src, g.at[pl.ds(ta, tb), place])
        out[:, half:] = jnp.zeros((ta + tb, lanes - half), BF16)
        for group, rows in ((early, slice(0, ta)), (late, slice(ta, ta + tb))):
            for copy in group:
                copy.wait()
            out[rows, :half] = lax.dot_general(
                g[rows], w[...], dims, preferred_element_type=F32
            ).astype(BF16)

    there = pl.BlockSpec(memory_space=pl.ANY)
    return pl.pallas_call(
        kernel,
        out_shape=jax.ShapeDtypeStruct((ta + tb, lanes), BF16),
        in_specs=[pl.BlockSpec(memory_space=pltpu.SMEM)] + [there] * 11,
        out_specs=pl.BlockSpec(memory_space=pltpu.VMEM),
        scratch_shapes=[
            pltpu.VMEM((ta + tb, 2 * deep), BF16),
            pltpu.VMEM((half, 2 * deep), BF16),
            pltpu.SemaphoreType.DMA((5 * Z,)),
        ],
        compiler_params=params(60),
        cost_estimate=SMALL,
    )(where, *ga, *gbs[0], *gbs[1], weights)


def cross(array, k):
    pairs = [(p * 2 + q, q * 2 + (p ^ k)) for p in range(2) for q in range(2)]
    return lax.ppermute(array, ("yh", "c"), pairs)


def shards(hidden, grad_out, weight):
    z, yh, x, yl, c = (lax.axis_index(name) for name in FINE)
    low, first = yh == 0, c == 0
    tokens, units = hidden.shape
    half = units // 2
    width = weight.shape[1]
    part = tokens // 3
    odd = z % 2 == 1

    a, b = grad_out[:part], grad_out[part:]
    b1, b3 = swap(b, Y, 1), swap(b, Y, 3)
    w_keep = pick(low, weight[:half], weight[half:])
    w_send = pick(low, weight[half:], weight[:half])
    b2 = swap(jnp.concatenate([b, w_send], axis=0), Y, 2)
    b2, w_pair = b2[: tokens - part], b2[tokens - part :]
    a1, a3 = swap(a, "x", 1), swap(a, "x", 3)
    a2 = swap(tie(a, a1), "x", 2)
    ht = hidden.T
    h_keep, h_send = pick(low, ht[:half], ht[half:]), pick(low, ht[half:], ht[:half])
    a, a1, a2, a3, b, b1, b2, b3, h_keep, h_send, w_keep, w_pair = (
        lax.optimization_barrier(
            (a, a1, a2, a3, b, b1, b2, b3, h_keep, h_send, w_keep, w_pair)
        )
    )

    ga0 = jnp.concatenate([a, a1, a2, a3], axis=1)
    gb0 = jnp.concatenate(
        [jnp.concatenate([b, b1], axis=1), jnp.concatenate([b2, b3], axis=1)], axis=0
    )
    gb1, gb3 = swap(gb0, "x", 1), swap(gb0, "x", 3)
    ga1, ga3 = swap(ga0, Y, 1), swap(ga0, Y, 3)
    h_got = swap(h_send, "yh", 1)
    same = yh == c
    mine = jnp.stack([pick(same, w_keep, w_pair), pick(same, w_pair, w_keep)])
    rows = lax.all_gather(mine, "z", axis=0, tiled=True)
    ga0, ga1, ga3, gb0, gb1, gb3, h_keep, h_got = lax.optimization_barrier(
        (ga0, ga1, ga3, gb0, gb1, gb3, h_keep, h_got)
    )

    cut = tokens - part
    gb2 = (swap(gb1[:cut], "x", 3), swap(gb3[cut:], "x", 1))
    ga2 = swap(ga0, Y, 2)
    h_own = jnp.concatenate(
        [h_keep[:, :part], h_got[:, :part], h_keep[:, part:], h_got[:, part:]], axis=1
    )
    h_other = swap(h_own, "c", 1)
    ga2, gb2, h_other = lax.optimization_barrier((ga2, gb2, h_other))
    straight = first != odd
    ht = jnp.concatenate(
        [pick(straight, h_own, h_other), pick(straight, h_other, h_own)], axis=0
    )
    ga = jnp.stack([ga0, ga1, ga2, ga3])
    gbs = [gb0, gb1, gb2, gb3]

    me = 2 * x + yl

    def places(xs):
        owner = me ^ jnp.array([2 * xs, 2 * xs + 1], jnp.int32)
        return (jnp.where(odd, z - owner, owner - z) + Z).astype(jnp.int32) % Z

    term = None
    for xs in (0, 1, 3, 2):
        term = terms(term, ht, ga, gbs[xs], xs, places(xs))

    ga_other, gbs_other = jax.tree.map(lambda piece: swap(piece, "c", 1), (ga, gbs))
    term, ga_other, gbs_other = lax.optimization_barrier((term, ga_other, gbs_other))

    owners = me ^ jnp.arange(Z, dtype=jnp.int32)
    lanes = -(-half // 128) * 128

    def step_on(step, got):
        new = [
            [
                hop(term, [5 - step, 4 + step][p] - h, h, got[1 - p][1 - h])
                for h in range(2)
            ]
            for p in range(2)
        ]
        return new, [[exchange(new[p][h], p) for h in range(2)] for p in range(2)]

    product = functools.partial(
        hidden_product, (ga, ga_other), (gbs, gbs_other), rows, lanes=lanes
    )
    _, got = step_on(1, [[None, None], [None, None]])
    _, got = step_on(2, got)
    new, got = step_on(3, got)
    gh_send = product(where=tie(owners, new), block=1)
    got = tie(got, gh_send)
    sent = [hop(term, 1, 0, got[1][1]), hop(term, 7, 1, got[0][0])]
    four = [exchange(sent[p], p) for p in range(2)]
    gh_got = swap(gh_send, "yh", 1)

    q0, q1 = last(term, got, four)
    straight = low != odd
    q0, q1 = pick(straight, q0, q1), pick(straight, q1, q0)
    gh_keep = product(where=tie(owners, q0, q1), block=0)
    q0, q1 = cross(q0, 0), cross(q1, 1)
    grad_weight = jnp.concatenate([pick(first, q0, q1), pick(first, q1, q0)], axis=0)

    gh_keep, gh_got = gh_keep[:, :half], gh_got[:, :half]
    grad_hidden = jnp.concatenate(
        [pick(low, gh_keep, gh_got), pick(low, gh_got, gh_keep)], axis=1
    )

    return (grad_hidden, grad_weight)


def solution(mesh):
    fine = Mesh(mesh.devices.reshape(Z, 2, 4, 2, 2), FINE)
    dp, tensor = FINE[:2], FINE[2:]
    return jax.shard_map(
        shards,
        mesh=fine,
        in_specs=(P(dp, tensor), P(dp, tensor), P(tensor, dp)),
        out_specs=(P(dp, tensor), P(tensor, dp)),
        check_vma=False,
    )
```

```python
import functools

import jax
import jax.numpy as jnp
from jax import lax
from jax.experimental import pallas as pl
from jax.experimental.pallas import tpu as pltpu
from jax.sharding import Mesh, PartitionSpec as P

FINE = ("z", "yh", "x", "yl", "c")
SIZE = {"z": 8, "x": 4, ("yh", "yl"): 4, "yh": 2, "c": 2, ("z", "yh"): 16}
Y = ("yh", "yl")
Z = 8
EXTRA = 16
SPREAD = 2.0**7.875
MIB = 2**20
F32 = jnp.float32
BF16 = jnp.bfloat16


def swap(array, axis, by):
    return lax.ppermute(array, axis, [(i, i ^ by) for i in range(SIZE[axis])])


def pick(first, a, b):
    return jnp.where(first, a, b)


def tie(values, *after):
    return lax.optimization_barrier((values, after))[0]


def params(mib):
    return pltpu.CompilerParams(vmem_limit_bytes=mib * MIB)


SMALL = pl.CostEstimate(flops=1000, bytes_accessed=1000, transcendentals=0)


def decode(code, e):
    code = code.astype(F32)
    root = lax.rsqrt(lax.rsqrt(lax.rsqrt(lax.rsqrt(jnp.abs(code)))))
    return jnp.where(code < 0, -root, root) * (jnp.exp2(e.astype(F32)) * (1 / SPREAD))


def decode_ref(ref, rows):
    return decode(ref[:rows], ref[rows : rows + 1])


def encode_ref(ref, total):
    rows = total.shape[0]
    top = jnp.max(jnp.abs(total), axis=0, keepdims=True)
    e = jnp.ceil(jnp.log2(jnp.maximum(top, 1e-30)))
    u = total * (jnp.exp2(-e) * SPREAD)
    u2 = u * u
    u4 = u2 * u2
    u8 = u4 * u4
    u16 = u8 * u8
    ref[:rows] = jnp.where(total < 0, -u16, u16).astype(BF16)
    ref[rows:] = jnp.broadcast_to(e, (EXTRA, total.shape[1])).astype(BF16)


PAIRING = (
    [(0, 1), (1, 0), (2, 3), (3, 2), (4, 5), (5, 4), (6, 7), (7, 6)],
    [(1, 2), (2, 1), (3, 4), (4, 3), (5, 6), (6, 5), (7, 0), (0, 7)],
)


def ring_call(kernel, term, picks, got, out_rows, n_out):
    rows, width = term.shape[1] // 2, term.shape[2]
    specs = [
        pl.BlockSpec((1, rows, width), lambda i, at=at: (at[0], at[1], 0))
        for at in picks
    ] + [pl.BlockSpec(g.shape, lambda i: (0, 0)) for g in got]
    out = jax.ShapeDtypeStruct((out_rows, width), BF16)
    return pl.pallas_call(
        kernel,
        out_shape=(out,) * n_out,
        grid=(1,),
        in_specs=specs,
        out_specs=[pl.BlockSpec(out.shape, lambda i: (0, 0))] * n_out,
        compiler_params=params(8),
        cost_estimate=SMALL,
    )(*[term] * len(picks), *got)


def hop(term, slot, half, got):
    rows = term.shape[1] // 2

    def kernel(t, *refs):
        total = t[0]
        if got is not None:
            total = total + decode_ref(refs[0], rows)
        encode_ref(refs[-1], total)

    got_ = [] if got is None else [got]
    return ring_call(kernel, term, [(slot, half)], got_, rows + EXTRA, 1)[0]


def last(term, three, four):
    rows = term.shape[1] // 2

    def kernel(t0, t1, a0, b1, f0, f1, o0, o1):
        o0[...] = (t0[0] + decode_ref(a0, rows) + decode_ref(f1, rows)).astype(BF16)
        o1[...] = (t1[0] + decode_ref(b1, rows) + decode_ref(f0, rows)).astype(BF16)

    got = [three[0][1], three[1][0], *four]
    return ring_call(kernel, term, [(0, 0), (0, 1)], got, rows, 2)


def exchange(array, pairing):
    return lax.ppermute(array, "z", PAIRING[pairing])


def terms(buffer, ht, ga, gb, xs, places):
    rows = ht.shape[0]
    gb = gb if isinstance(gb, tuple) else (gb,)
    ta, width = ga.shape[1], gb[0].shape[1] // 2

    def kernel(s, *refs):
        ht_ref, own, pair, *b, out = refs[len(first) :]
        g = jnp.concatenate([own[0], pair[0]] + [part[...] for part in b], axis=0)
        out[0] = jnp.dot(ht_ref[...], g, preferred_element_type=F32)

    first = [] if buffer is None else [buffer]
    return pl.pallas_call(
        kernel,
        out_shape=jax.ShapeDtypeStruct((Z, rows, width), F32),
        grid_spec=pltpu.PrefetchScalarGridSpec(
            num_scalar_prefetch=1,
            grid=(2,),
            in_specs=[pl.BlockSpec(memory_space=pl.ANY) for _ in first]
            + [
                pl.BlockSpec(ht.shape, lambda i, s: (0, 0)),
                pl.BlockSpec((1, ta, width), lambda i, s: (i, 0, xs)),
                pl.BlockSpec((1, ta, width), lambda i, s: (2 + i, 0, xs)),
            ]
            + [pl.BlockSpec((b.shape[0], width), lambda i, s: (0, i)) for b in gb],
            out_specs=pl.BlockSpec((1, rows, width), lambda i, s: (s[i], 0, 0)),
        ),
        input_output_aliases={} if buffer is None else {1: 0},
        compiler_params=params(24),
        cost_estimate=SMALL,
    )(places, *first, ht, ga, ga, *gb)


def hidden_product(ga, gbs, weights, where, lanes, block):
    half, width = weights.shape[1:]
    ta, tb = ga[0].shape[1], gbs[0][0].shape[0] // 2
    gbs = [[g[block] if isinstance(g, tuple) else g for g in core] for core in gbs]
    deep = Z * width
    dims = (((1,), (1,)), ((), ()))

    def kernel(s, *refs):
        a_refs, b_refs, w_ref, (out, g, w, sems) = refs[:2], refs[2:10], refs[10], refs[11:]
        early, late = [], []

        def fetch(group, src, dst):
            copy = pltpu.make_async_copy(src, dst, sems.at[len(early) + len(late)])
            copy.start()
            group.append(copy)

        for core in range(2):
            for k in range(Z):
                place = pl.ds(core * deep + k * width, width)
                fetch(early, w_ref.at[2 * s[k] + core], w.at[:, place])
                src = a_refs[core].at[2 * block + k % 2, :, pl.ds(k // 2 * width, width)]
                fetch(early, src, g.at[pl.ds(0, ta), place])
        for core in range(2):
            for k in range(Z // 2):
                place = pl.ds(core * deep + k * 2 * width, 2 * width)
                src = b_refs[core * 4 + k]
                if src.shape[0] > tb:
                    src = src.at[pl.ds(block * tb, tb)]
                fetch(late, src, g.at[pl.ds(ta, tb), place])
        out[:, half:] = jnp.zeros((ta + tb, lanes - half), BF16)
        for group, rows in ((early, slice(0, ta)), (late, slice(ta, ta + tb))):
            for copy in group:
                copy.wait()
            out[rows, :half] = lax.dot_general(
                g[rows], w[...], dims, preferred_element_type=F32
            ).astype(BF16)

    there = pl.BlockSpec(memory_space=pl.ANY)
    return pl.pallas_call(
        kernel,
        out_shape=jax.ShapeDtypeStruct((ta + tb, lanes), BF16),
        in_specs=[pl.BlockSpec(memory_space=pltpu.SMEM)] + [there] * 11,
        out_specs=pl.BlockSpec(memory_space=pltpu.VMEM),
        scratch_shapes=[
            pltpu.VMEM((ta + tb, 2 * deep), BF16),
            pltpu.VMEM((half, 2 * deep), BF16),
            pltpu.SemaphoreType.DMA((5 * Z,)),
        ],
        compiler_params=params(51),
        cost_estimate=SMALL,
    )(where, *ga, *gbs[0], *gbs[1], weights)


def cross(array, k):
    pairs = [(p * 2 + q, q * 2 + (p ^ k)) for p in range(2) for q in range(2)]
    return lax.ppermute(array, ("yh", "c"), pairs)


def shards(hidden, grad_out, weight):
    z, yh, x, yl, c = (lax.axis_index(name) for name in FINE)
    low, first = yh == 0, c == 0
    tokens, units = hidden.shape
    half = units // 2
    width = weight.shape[1]
    part = tokens // 3
    odd = z % 2 == 1

    a, b = grad_out[:part], grad_out[part:]
    b1, b3 = swap(b, Y, 1), swap(b, Y, 3)
    w_keep = pick(low, weight[:half], weight[half:])
    w_send = pick(low, weight[half:], weight[:half])
    b2 = swap(jnp.concatenate([b, w_send], axis=0), Y, 2)
    b2, w_pair = b2[: tokens - part], b2[tokens - part :]
    a1, a3 = swap(a, "x", 1), swap(a, "x", 3)
    a2 = swap(tie(a, a1), "x", 2)
    ht = hidden.T
    h_keep, h_send = pick(low, ht[:half], ht[half:]), pick(low, ht[half:], ht[:half])
    a, a1, a2, a3, b, b1, b2, b3, h_keep, h_send, w_keep, w_pair = (
        lax.optimization_barrier(
            (a, a1, a2, a3, b, b1, b2, b3, h_keep, h_send, w_keep, w_pair)
        )
    )

    ga0 = jnp.concatenate([a, a1, a2, a3], axis=1)
    gb0 = jnp.concatenate(
        [jnp.concatenate([b, b1], axis=1), jnp.concatenate([b2, b3], axis=1)], axis=0
    )
    gb1, gb3 = swap(gb0, "x", 1), swap(gb0, "x", 3)
    ga1, ga3 = swap(ga0, Y, 1), swap(ga0, Y, 3)
    h_got = swap(h_send, "yh", 1)
    same = yh == c
    mine = jnp.stack([pick(same, w_keep, w_pair), pick(same, w_pair, w_keep)])
    rows = lax.all_gather(mine, "z", axis=0, tiled=True)
    ga0, ga1, ga3, gb0, gb1, gb3, h_keep, h_got = lax.optimization_barrier(
        (ga0, ga1, ga3, gb0, gb1, gb3, h_keep, h_got)
    )

    cut = tokens - part
    gb2 = (swap(gb1[:cut], "x", 3), swap(gb3[cut:], "x", 1))
    ga2 = swap(ga0, Y, 2)
    h_own = jnp.concatenate(
        [h_keep[:, :part], h_got[:, :part], h_keep[:, part:], h_got[:, part:]], axis=1
    )
    h_other = swap(h_own, "c", 1)
    ga2, gb2, h_other = lax.optimization_barrier((ga2, gb2, h_other))
    straight = first != odd
    ht = jnp.concatenate(
        [pick(straight, h_own, h_other), pick(straight, h_other, h_own)], axis=0
    )
    ga = jnp.stack([ga0, ga1, ga2, ga3])
    gbs = [gb0, gb1, gb2, gb3]

    me = 2 * x + yl

    def places(xs):
        owner = me ^ jnp.array([2 * xs, 2 * xs + 1], jnp.int32)
        return (jnp.where(odd, z - owner, owner - z) + Z).astype(jnp.int32) % Z

    term = None
    for xs in (0, 1, 3, 2):
        term = terms(term, ht, ga, gbs[xs], xs, places(xs))

    ga_other, gbs_other = jax.tree.map(lambda piece: swap(piece, "c", 1), (ga, gbs))
    term, ga_other, gbs_other = lax.optimization_barrier((term, ga_other, gbs_other))

    owners = me ^ jnp.arange(Z, dtype=jnp.int32)
    lanes = -(-half // 128) * 128

    def step_on(step, got):
        new = [
            [
                hop(term, [5 - step, 4 + step][p] - h, h, got[1 - p][1 - h])
                for h in range(2)
            ]
            for p in range(2)
        ]
        return new, [[exchange(new[p][h], p) for h in range(2)] for p in range(2)]

    product = functools.partial(
        hidden_product, (ga, ga_other), (gbs, gbs_other), rows, lanes=lanes
    )
    _, got = step_on(1, [[None, None], [None, None]])
    _, got = step_on(2, got)
    new, got = step_on(3, got)
    gh_send = product(where=tie(owners, new), block=1)
    got = tie(got, gh_send)
    sent = [hop(term, 1, 0, got[1][1]), hop(term, 7, 1, got[0][0])]
    four = [exchange(sent[p], p) for p in range(2)]
    gh_got = swap(gh_send, "yh", 1)

    q0, q1 = last(term, got, four)
    straight = low != odd
    q0, q1 = pick(straight, q0, q1), pick(straight, q1, q0)
    gh_keep = product(where=tie(owners, q0, q1), block=0)
    q0, q1 = cross(q0, 0), cross(q1, 1)
    grad_weight = jnp.concatenate([pick(first, q0, q1), pick(first, q1, q0)], axis=0)

    gh_keep, gh_got = gh_keep[:, :half], gh_got[:, :half]
    grad_hidden = jnp.concatenate(
        [pick(low, gh_keep, gh_got), pick(low, gh_got, gh_keep)], axis=1
    )

    return (grad_hidden, grad_weight)


def solution(mesh):
    fine = Mesh(mesh.devices.reshape(Z, 2, 4, 2, 2), FINE)
    dp, tensor = FINE[:2], FINE[2:]
    return jax.shard_map(
        shards,
        mesh=fine,
        in_specs=(P(dp, tensor), P(dp, tensor), P(tensor, dp)),
        out_specs=(P(dp, tensor), P(tensor, dp)),
        check_vma=False,
    )
```
